32 devices in a mesh: feat: 16 (over z, x, core), node: 2 (over y).
Axes of the slice: x: 2, y: 2, z: 4, core: 2. Of those that a mesh axis runs over, the one named last changes fastest.
Arguments:
- feats: bfloat16 [1024, 8192], P('feat', 'node'), may hold values from -6 to 6
- weight: bfloat16 [1024, 256], replicated, may hold values from -0.1875 to 0.1875
- tile_row: int32 [16, 2, 8], P('feat', 'node'), may hold values from 0 to 1, as said below
- tile_col: int32 [16, 2, 8], P('feat', 'node'), may hold values from 0 to 3
- tile_block: int32 [16, 2, 8], P('feat', 'node'), may hold values from 0 to 7, each once within a row
- tile_count: int32 [16, 2], P('feat', 'node'), may hold values from 2 to 8, as said below
- edge_blocks: bfloat16 [16, 2, 8, 128, 128], P('feat', 'node'), may hold values from -0.375 to 0.375
- cotangent: bfloat16 [256, 8192], P(None, ('node', 'feat')), may hold values from -0.06591797 to 0.06591797
Outputs:
- act: bfloat16 [256, 8192], P(None, ('node', 'feat'))
- weight_grad: float32 [1024, 256], P(('feat', 'node'))
The draws below stay inside these ranges and needn't reach their ends.
Inputs may be any that keep to these rules, and one draw needn't show every extreme that they name: Within one device block the pairs (tile_row, tile_col) of its 8 slots name every tile position once. Within one device block tile_block names each of its 8 blocks once. Slots s at or after tile_count of their block are unused; some block uses all 8 slots.
All inputs are finite; a program needn't handle non-finite values.
Results may differ from the reference program's by a relative error of at most 0.012.
Values may be sent and summed in bfloat16 or wider, within the bound.
No kernel may reach another device: no remote copies, remote signals or barrier semaphores. Data moves between devices by JAX's collectives and lax.ppermute only.
A program may use at most 64 MiB of HBM per device.

```python
import jax
import jax.numpy as jnp
from jax import lax

FIN = 1024
HID = 256
TILE = 128
RT_DEV = 2
ROWS = 256
NODES = 8192
CLUSTER = 512
SLOTS = 8
N_FEAT = 16
N_NODE = 2


def tile_positions(key):
    keys = jax.random.split(jax.random.fold_in(key, 17), N_FEAT * N_NODE)
    orders = jax.vmap(lambda single: jax.random.permutation(single, SLOTS))(keys)
    return orders.astype(jnp.int32).reshape(N_FEAT, N_NODE, SLOTS)


def draw_tile_row(key, part):
    return (tile_positions(key) // (N_NODE * RT_DEV)).astype(jnp.int32)


def draw_tile_col(key, part):
    return (tile_positions(key) % (N_NODE * RT_DEV)).astype(jnp.int32)


def draw_tile_count(key, part):
    levels = jax.random.randint(jax.random.fold_in(key, 5), (N_FEAT * N_NODE,), 0, 3)
    divisor = jnp.where(levels == 0, 1, jnp.where(levels == 1, 2, 4))
    counts = SLOTS // divisor
    busiest = jax.random.randint(jax.random.fold_in(key, 9), (), 0, N_FEAT * N_NODE)
    counts = counts.at[busiest].set(SLOTS)
    return counts.astype(jnp.int32).reshape(N_FEAT, N_NODE)


def shard_levels(key, dims, pieces, least, largest):
    factor_of = 1.0
    for axis_at, parts in pieces:
        draws = jax.random.uniform(jax.random.fold_in(jax.random.fold_in(key, 6), axis_at), (parts,), jnp.float32, least / len(pieces), largest / len(pieces))
        factor_of = factor_of * jnp.repeat(jnp.exp(draws), dims[axis_at] // parts).reshape((-1,) + (1,) * (len(dims) - 1 - axis_at))
    return factor_of


def scatter_about(key, shape, deviation, bound, shards=(), kind=jnp.bfloat16):
    drawn = jax.random.normal(key, shape, jnp.float32) * deviation
    if len(shards) > 0:
        drawn = shard_levels(key, shape, shards, -0.22, 0.18) * drawn
    return jnp.clip(drawn, min=-bound, max=bound).astype(kind)


def setup_inputs(seed: int = 0) -> dict:
    arg_keys = jax.random.split(jax.random.key(seed), 9)
    return {
        "feats": scatter_about(arg_keys[0], (FIN, NODES), 1.0, 6.0, ((0, 16), (1, 2))),
        "weight": scatter_about(arg_keys[1], (FIN, HID), FIN ** -0.5, 0.1875),
        "tile_row": draw_tile_row(jax.random.fold_in(arg_keys[8], 71), 0),
        "tile_col": draw_tile_col(jax.random.fold_in(arg_keys[8], 71), 0),
        "tile_block": jax.vmap(lambda own: jax.random.permutation(own, SLOTS))(jax.random.split(arg_keys[4], N_FEAT * N_NODE)).reshape((N_FEAT, N_NODE, SLOTS)).astype(jnp.int32),
        "tile_count": draw_tile_count(jax.random.fold_in(arg_keys[8], 71), 0),
        "edge_blocks": scatter_about(arg_keys[6], (N_FEAT, N_NODE, SLOTS, TILE, TILE), (TILE * RT_DEV * N_NODE // 2) ** -0.5, 0.375, ((0, 16), (1, 2))),
        "cotangent": scatter_about(arg_keys[7], (HID, NODES), (NODES ** -0.5), 0.06591797, ((1, 32),)),
    }


root_half = 0.7071067811865476
inv_root_two_pi = 0.3989422804014327


def dense_adjacency(row_tile, col_tile, block_index, live_count, blocks, row_tiles, col_tiles):
    slot_total = row_tile.shape[0]
    tile_size = blocks.shape[-1]
    position = row_tile * col_tiles + col_tile
    places = jnp.arange(row_tiles * col_tiles, dtype=jnp.int32)
    active = jnp.arange(slot_total, dtype=jnp.int32) < live_count
    matches = (position[None, :] == places[:, None]) & active[None, :]
    chosen = jnp.sum(jnp.where(matches, block_index[None, :], 0), axis=1).astype(jnp.int32)
    filled = jnp.any(matches, axis=1)
    picked = jnp.take(blocks, chosen, axis=0) * filled[:, None, None].astype(blocks.dtype)
    layout = picked.reshape(row_tiles, col_tiles, tile_size, tile_size)
    return layout.transpose(0, 2, 1, 3).reshape(row_tiles * tile_size, col_tiles * tile_size)


def gelu_parts(preact):
    normal_cdf = 0.5 * (1.0 + lax.erf(preact * root_half))
    normal_pdf = jnp.exp(-0.5 * preact * preact) * inv_root_two_pi
    return preact * normal_cdf, normal_cdf + preact * normal_pdf


def reference(feats, weight, tile_row, tile_col, tile_block, tile_count, edge_blocks, cotangent):
    projected = jnp.dot(weight.T, feats, preferred_element_type=jnp.float32)
    proj_four = projected.reshape(HID, N_NODE, N_FEAT, ROWS)
    cot_four = cotangent.reshape(HID, N_NODE, N_FEAT, ROWS)

    def per_cluster(fidx):
        cluster_proj = proj_four[:, :, fidx, :].reshape(HID, CLUSTER)

        def per_block(nidx):
            adjacency = dense_adjacency(tile_row[fidx, nidx], tile_col[fidx, nidx], tile_block[fidx, nidx],
                                        tile_count[fidx, nidx], edge_blocks[fidx, nidx], RT_DEV,
                                        N_NODE * RT_DEV).astype(jnp.float32)
            preact = jnp.dot(cluster_proj, adjacency.T, precision=lax.Precision.HIGHEST)
            output, derivative = gelu_parts(preact)
            pre_grad = cot_four[:, nidx, fidx, :].astype(jnp.float32) * derivative
            node_terms = jnp.dot(adjacency.T, pre_grad.T, precision=lax.Precision.HIGHEST)
            return output.astype(jnp.bfloat16), node_terms

        outputs, node_terms = lax.map(per_block, jnp.arange(N_NODE, dtype=jnp.int32))
        return outputs, jnp.sum(node_terms, axis=0)

    outputs, node_sums = lax.map(per_cluster, jnp.arange(N_FEAT, dtype=jnp.int32))
    act = outputs.transpose(2, 1, 0, 3).reshape(HID, NODES)
    node_grad = node_sums.reshape(N_FEAT, N_NODE, ROWS, HID).transpose(1, 0, 2, 3).reshape(NODES, HID)
    weight_grad = jnp.dot(feats.astype(jnp.float32), node_grad, precision=lax.Precision.HIGHEST)
    return act, weight_grad
```

```python
import jax
import jax.numpy as jnp
from jax import lax
from jax.sharding import Mesh, PartitionSpec as P

root_half = 0.7071067811865476
inv_root_two_pi = 0.3989422804014327

SWAP = ((0, 1), (1, 0))
TRANSPOSE = ((0, 0), (1, 2), (2, 1), (3, 3))


def dense_adjacency(row_tile, col_tile, block_index, live_count, blocks, row_tiles, col_tiles):
    slot_total = row_tile.shape[0]
    tile_size = blocks.shape[-1]
    position = row_tile * col_tiles + col_tile
    places = jnp.arange(row_tiles * col_tiles, dtype=jnp.int32)
    active = jnp.arange(slot_total, dtype=jnp.int32) < live_count
    matches = (position[None, :] == places[:, None]) & active[None, :]
    chosen = jnp.sum(jnp.where(matches, block_index[None, :], 0), axis=1)
    filled = jnp.any(matches, axis=1)
    picked = jnp.take(blocks, chosen, axis=0) * filled[:, None, None].astype(blocks.dtype)
    layout = picked.reshape(row_tiles, col_tiles, tile_size, tile_size)
    return layout.transpose(0, 2, 1, 3).reshape(row_tiles * tile_size, col_tiles * tile_size)


def gelu_parts(preact):
    normal_cdf = 0.5 * (1.0 + lax.erf(preact * root_half))
    normal_pdf = jnp.exp(-0.5 * preact * preact) * inv_root_two_pi
    return (preact * normal_cdf, normal_cdf + preact * normal_pdf)


def dot(left, right, left_dim, right_dim):
    return lax.dot_general(
        left, right, (((left_dim,), (right_dim,)), ((), ())), preferred_element_type=jnp.float32
    )


def per_device(feats, weight, tile_row, tile_col, tile_block, tile_count, edge_blocks, cotangent):
    columns = lax.axis_size("col")
    pairs = lax.axis_size("hi")
    core = lax.axis_index("core")
    width, shard_nodes = feats.shape
    rows = shard_nodes // (2 * columns)
    hidden = weight.shape[1]
    tile_size = edge_blocks.shape[-1]
    row_tiles = rows // tile_size
    slot_total = edge_blocks.shape[2]
    bf16 = jnp.bfloat16

    by_dest = feats.reshape(width, 2 * columns, rows)
    arrived = lax.all_to_all(by_dest, ("col", "lo"), split_axis=1, concat_axis=0, tiled=True)
    arrived = arrived.reshape(columns, 2, width, rows)

    adjacency = dense_adjacency(
        tile_row[0, 0], tile_col[0, 0], tile_block[0, 0], tile_count[0, 0], edge_blocks[0, 0],
        row_tiles, slot_total // row_tiles,
    )
    adjacency = lax.ppermute(adjacency, ("core", "lo"), TRANSPOSE)
    cot = lax.ppermute(cotangent, ("core", "lo"), TRANSPOSE)

    own_weight = lax.dynamic_index_in_dim(
        weight.reshape(columns, 2, width, hidden), core, 1, keepdims=False
    ).reshape(columns * width, hidden)
    nodes = arrived.transpose(0, 2, 1, 3).reshape(columns * width, 2 * rows)
    part = dot(own_weight, nodes, 0, 0)
    other = lax.ppermute(part.astype(bf16), "core", SWAP)
    projected = (part + other.astype(jnp.float32)).astype(bf16)
    if pairs > 1:
        projected = lax.all_gather(projected, "hi", axis=1, tiled=True)
    preact = dot(projected, adjacency, 1, 1)
    output, derivative = gelu_parts(preact)
    pre_grad = (cot.astype(jnp.float32) * derivative).astype(bf16)
    node_part = dot(pre_grad, adjacency, 1, 0)
    if pairs > 1:
        node_part = lax.psum_scatter(node_part, "hi", scatter_dimension=1, tiled=True)
    node_other = lax.ppermute(node_part.astype(bf16), "core", SWAP)
    node_grad = (node_part + node_other.astype(jnp.float32)).astype(bf16)
    terms = dot(nodes, node_grad, 1, 1)
    share = width // (2 * pairs)
    if pairs > 1:
        terms = terms.reshape(columns, pairs, 2 * share, hidden)
        terms = lax.psum_scatter(terms, "hi", scatter_dimension=1, tiled=True)
    terms = terms.astype(bf16).reshape(2 * columns, share, hidden)
    act = lax.ppermute(output.astype(bf16), ("core", "lo"), TRANSPOSE)
    terms = lax.all_to_all(terms, ("col", "lo"), split_axis=0, concat_axis=0, tiled=True)
    weight_grad = jnp.sum(terms.astype(jnp.float32), axis=0)
    return (act, weight_grad)


def solution(mesh):
    n_feat, n_node = mesh.shape["feat"], mesh.shape["node"]
    fine = Mesh(
        mesh.devices.reshape(n_feat // 2, 2, n_node // 2, 2), ("col", "core", "hi", "lo")
    )
    feat, node = ("col", "core"), ("hi", "lo")
    return jax.shard_map(
        per_device,
        mesh=fine,
        in_specs=(
            P(feat, node),
            P(),
            P(feat, node, None),
            P(feat, node, None),
            P(feat, node, None),
            P(feat, node),
            P(feat, node, None, None, None),
            P(None, node + feat),
        ),
        out_specs=(P(None, node + feat), P(feat + node, None)),
        check_vma=False,
    )
```

```python
import functools

import jax
import jax.numpy as jnp
from jax import lax
from jax.experimental import pallas as pl
from jax.experimental.pallas import tpu as pltpu
from jax.sharding import Mesh, PartitionSpec as P

root_half = 0.7071067811865476
inv_root_two_pi = 0.3989422804014327

SWAP = ((0, 1), (1, 0))
TRANSPOSE = ((0, 0), (1, 2), (2, 1), (3, 3))
VMEM = pl.BlockSpec(memory_space=pltpu.VMEM)
SMEM = pl.BlockSpec(memory_space=pltpu.SMEM)
ANY = pl.BlockSpec(memory_space=pl.ANY)
PARAMS = pltpu.CompilerParams(vmem_limit_bytes=24 * 1024 * 1024)


def dot(left, right, left_dim, right_dim):
    return lax.dot_general(
        left, right, (((left_dim,), (right_dim,)), ((), ())), preferred_element_type=jnp.float32
    )


def chunk_kernel(feats, chunks, sems):
    count, _, rows = chunks.shape
    copies = [
        pltpu.make_async_copy(feats.at[:, pl.ds(at * rows, rows)], chunks.at[at], sems.at[at])
        for at in range(count)
    ]
    for copy in copies:
        copy.start()
    for copy in copies:
        copy.wait()


def by_destination(feats, count):
    width, nodes = feats.shape
    return pl.pallas_call(
        chunk_kernel,
        out_shape=jax.ShapeDtypeStruct((count, width, nodes // count), feats.dtype),
        in_specs=[ANY],
        out_specs=ANY,
        scratch_shapes=[pltpu.SemaphoreType.DMA((count,))],
        compiler_params=PARAMS,
        name="by_destination",
    )(feats)


def adjacency_kernel(row_tile, col_tile, block_index, live, blocks, out):
    slots, tile, _ = blocks.shape
    for slot in range(slots):
        row = pl.multiple_of(row_tile[slot] * tile, tile)
        col = pl.multiple_of(col_tile[slot] * tile, tile)
        block = blocks[block_index[slot]]
        out[pl.ds(row, tile), pl.ds(col, tile)] = jnp.where(
            slot < live[0], block, jnp.zeros_like(block)
        )


def dense_adjacency(row_tile, col_tile, block_index, live, blocks, rows):
    slots, tile, _ = blocks.shape
    return pl.pallas_call(
        adjacency_kernel,
        out_shape=jax.ShapeDtypeStruct((rows, slots * tile * tile // rows), blocks.dtype),
        in_specs=[SMEM, SMEM, SMEM, SMEM, VMEM],
        out_specs=VMEM,
        compiler_params=PARAMS,
        name="dense_adjacency",
    )(row_tile, col_tile, block_index, live, blocks)


def project_kernel(weight, arrived, part, part_out):
    columns, places, width, rows = arrived.shape
    for place in range(places):
        nodes = arrived[:, place].reshape(columns * width, rows)
        value = dot(weight[...], nodes, 1, 0)
        part[:, place * rows : (place + 1) * rows] = value
        part_out[:, place * rows : (place + 1) * rows] = value.astype(part_out.dtype)


def project(weight, arrived):
    hidden = weight.shape[0]
    columns, places, width, rows = arrived.shape
    shape = (hidden, places * rows)
    return pl.pallas_call(
        project_kernel,
        out_shape=(
            jax.ShapeDtypeStruct(shape, jnp.float32),
            jax.ShapeDtypeStruct(shape, jnp.bfloat16),
        ),
        in_specs=[VMEM, VMEM],
        out_specs=(VMEM, VMEM),
        compiler_params=PARAMS,
        name="project",
    )(weight, arrived)


def block_kernel(*refs):
    *projected, adjacency, cotangent, act, terms, terms_out = refs
    if len(projected) == 2:
        part, other = projected
        nodes = (part[...] + other[...].astype(jnp.float32)).astype(jnp.bfloat16)
    else:
        nodes = projected[0][...]
    preact = dot(nodes, adjacency[...], 1, 1)
    normal_cdf = 0.5 * (1.0 + lax.erf(preact * root_half))
    normal_pdf = jnp.exp(-0.5 * preact * preact) * inv_root_two_pi
    act[...] = (preact * normal_cdf).astype(act.dtype)
    derivative = normal_cdf + preact * normal_pdf
    pre_grad = (cotangent[...].astype(jnp.float32) * derivative).astype(jnp.bfloat16)
    value = dot(pre_grad, adjacency[...], 1, 0)
    terms[...] = value
    terms_out[...] = value.astype(terms_out.dtype)


def block(projected, adjacency, cotangent):
    hidden, rows = cotangent.shape
    shape = (hidden, adjacency.shape[1])
    return pl.pallas_call(
        block_kernel,
        out_shape=(
            jax.ShapeDtypeStruct((hidden, rows), jnp.bfloat16),
            jax.ShapeDtypeStruct(shape, jnp.float32),
            jax.ShapeDtypeStruct(shape, jnp.bfloat16),
        ),
        in_specs=[VMEM] * (len(projected) + 2),
        out_specs=(VMEM,) * 3,
        compiler_params=PARAMS,
        name="block",
    )(*projected, adjacency, cotangent)


def gradient_kernel(arrived, part, other, terms):
    columns, places, width, rows = arrived.shape
    node_grad = (part[...] + other[...].astype(jnp.float32)).astype(jnp.bfloat16)
    total = None
    for place in range(places):
        nodes = arrived[:, place].reshape(columns * width, rows)
        value = dot(nodes, node_grad[:, place * rows : (place + 1) * rows], 1, 1)
        total = value if total is None else total + value
    terms[...] = total.astype(terms.dtype)


def gradient(arrived, part, other, dtype):
    columns, places, width, rows = arrived.shape
    return pl.pallas_call(
        gradient_kernel,
        out_shape=jax.ShapeDtypeStruct((columns * width, part.shape[0]), dtype),
        in_specs=[VMEM] * 3,
        out_specs=VMEM,
        compiler_params=PARAMS,
        name="gradient",
    )(arrived, part, other)


def per_device(feats, weight, tile_row, tile_col, tile_block, tile_count, edge_blocks, cotangent):
    columns = lax.axis_size("col")
    pairs = lax.axis_size("hi")
    core = lax.axis_index("core")
    width, shard_nodes = feats.shape
    rows = shard_nodes // (2 * columns)
    hidden = weight.shape[1]
    bf16 = jnp.bfloat16

    chunks = by_destination(feats, 2 * columns)
    arrived = lax.all_to_all(chunks, ("col", "lo"), split_axis=0, concat_axis=0, tiled=True)
    arrived = arrived.reshape(columns, 2, width, rows)

    cot = lax.ppermute(cotangent, ("core", "lo"), TRANSPOSE)
    adjacency = dense_adjacency(
        tile_row[0, 0], tile_col[0, 0], tile_block[0, 0], tile_count[0], edge_blocks[0, 0], rows
    )
    adjacency = lax.ppermute(adjacency, ("core", "lo"), TRANSPOSE)
    own_weight = lax.dynamic_index_in_dim(
        weight.reshape(columns, 2, width, hidden), core, 1, keepdims=False
    ).reshape(columns * width, hidden).T
    arrived, cot, adjacency, own_weight = lax.optimization_barrier(
        (arrived, cot, adjacency, own_weight)
    )

    part, sent = project(own_weight, arrived)
    other = lax.ppermute(sent, "core", SWAP)
    projected = (part, other)
    if pairs > 1:
        total = (part + other.astype(jnp.float32)).astype(bf16)
        projected = (lax.all_gather(total, "hi", axis=1, tiled=True),)
    output, part, sent = block(projected, adjacency, cot)
    if pairs > 1:
        part = lax.psum_scatter(part, "hi", scatter_dimension=1, tiled=True)
        sent = part.astype(bf16)
    other = lax.ppermute(sent, "core", SWAP)
    terms = gradient(arrived, part, other, jnp.float32 if pairs > 1 else bf16)
    share = width // (2 * pairs)
    if pairs > 1:
        terms = terms.reshape(columns, pairs, 2 * share, hidden)
        terms = lax.psum_scatter(terms, "hi", scatter_dimension=1, tiled=True).astype(bf16)
    terms = terms.reshape(2 * columns, share, hidden)
    act = lax.ppermute(output, ("core", "lo"), TRANSPOSE)
    terms = lax.all_to_all(terms, ("col", "lo"), split_axis=0, concat_axis=0, tiled=True)
    weight_grad = jnp.sum(terms.astype(jnp.float32), axis=0)
    return (act, weight_grad)


def solution(mesh):
    n_feat, n_node = mesh.shape["feat"], mesh.shape["node"]
    fine = Mesh(
        mesh.devices.reshape(n_feat // 2, 2, n_node // 2, 2), ("col", "core", "hi", "lo")
    )
    feat, node = ("col", "core"), ("hi", "lo")
    return jax.shard_map(
        per_device,
        mesh=fine,
        in_specs=(
            P(feat, node),
            P(),
            P(feat, node, None),
            P(feat, node, None),
            P(feat, node, None),
            P(feat, node),
            P(feat, node, None, None, None),
            P(None, node + feat),
        ),
        out_specs=(P(None, node + feat), P(feat + node, None)),
        check_vma=False,
    )
```

```python
import functools

import jax
import jax.numpy as jnp
from jax import lax
from jax.experimental import pallas as pl
from jax.experimental.pallas import tpu as pltpu
from jax.sharding import Mesh, PartitionSpec as P

root_half = 0.7071067811865476
inv_root_two_pi = 0.3989422804014327

SWAP = ((0, 1), (1, 0))
TRANSPOSE = ((0, 0), (1, 2), (2, 1), (3, 3))
VMEM = pl.BlockSpec(memory_space=pltpu.VMEM)
SMEM = pl.BlockSpec(memory_space=pltpu.SMEM)
ANY = pl.BlockSpec(memory_space=pl.ANY)
PARAMS = pltpu.CompilerParams(vmem_limit_bytes=24 * 1024 * 1024)


def dot(left, right, left_dim, right_dim):
    return lax.dot_general(
        left, right, (((left_dim,), (right_dim,)), ((), ())), preferred_element_type=jnp.float32
    )


def chunk_kernel(feats, chunks, held, in_sems, out_sems):
    places, columns, _, rows = chunks.shape
    spots = [(place, column) for column in range(columns) for place in range(places)]
    loads, stores = [], []
    for at, (place, column) in enumerate(spots):
        loads.append(
            pltpu.make_async_copy(
                feats.at[:, pl.ds(at * rows, rows)], held.at[place, column], in_sems.at[at]
            )
        )
        stores.append(
            pltpu.make_async_copy(held.at[place, column], chunks.at[place, column], out_sems.at[at])
        )
    for load in loads:
        load.start()
    for load, store in zip(loads, stores):
        load.wait()
        store.start()
    for store in stores:
        store.wait()


def by_destination(feats, places, columns):
    width, nodes = feats.shape
    shape = (places, columns, width, nodes // (places * columns))
    return pl.pallas_call(
        chunk_kernel,
        out_shape=jax.ShapeDtypeStruct(shape, feats.dtype),
        in_specs=[pl.BlockSpec(memory_space=pltpu.HBM)],
        out_specs=pl.BlockSpec(memory_space=pltpu.HBM),
        scratch_shapes=[
            pltpu.VMEM(shape, feats.dtype),
            pltpu.SemaphoreType.DMA((places * columns,)),
            pltpu.SemaphoreType.DMA((places * columns,)),
        ],
        compiler_params=pltpu.CompilerParams(vmem_limit_bytes=60 * 1024 * 1024),
        name="by_destination",
    )(feats)


def side_kernel(row_tile, col_tile, block_index, live, blocks, cotangent, out):
    slots, tile, _ = blocks.shape
    hidden, rows = cotangent.shape
    groups = out.shape[1] // rows
    part = hidden // groups
    for slot in range(slots):
        row = pl.multiple_of(row_tile[slot] * tile, tile)
        col = pl.multiple_of(col_tile[slot] * tile, tile)
        block = blocks[block_index[slot]]
        out[pl.ds(row, tile), pl.ds(col, tile)] = jnp.where(
            slot < live[0], block, jnp.zeros_like(block)
        )
    for group in range(groups):
        out[rows : rows + part, group * rows : (group + 1) * rows] = cotangent[
            group * part : (group + 1) * part, :
        ]


def side_inputs(row_tile, col_tile, block_index, live, blocks, cotangent):
    slots, tile, _ = blocks.shape
    hidden, rows = cotangent.shape
    cluster = slots * tile * tile // rows
    return pl.pallas_call(
        side_kernel,
        out_shape=jax.ShapeDtypeStruct((rows + hidden * rows // cluster, cluster), blocks.dtype),
        in_specs=[SMEM] * 4 + [VMEM] * 2,
        out_specs=VMEM,
        compiler_params=PARAMS,
        name="side_inputs",
    )(row_tile, col_tile, block_index, live, blocks, cotangent)


def project_kernel(weight, arrived, part, part_out):
    places, columns, width, rows = arrived.shape
    for place in range(places):
        nodes = arrived[place].reshape(columns * width, rows)
        value = dot(weight[...], nodes, 1, 0)
        part[:, place * rows : (place + 1) * rows] = value
        part_out[:, place * rows : (place + 1) * rows] = value.astype(part_out.dtype)


def project(weight, arrived):
    hidden = weight.shape[0]
    places, columns, width, rows = arrived.shape
    shape = (hidden, places * rows)
    return pl.pallas_call(
        project_kernel,
        out_shape=(
            jax.ShapeDtypeStruct(shape, jnp.float32),
            jax.ShapeDtypeStruct(shape, jnp.bfloat16),
        ),
        in_specs=[VMEM, VMEM],
        out_specs=(VMEM, VMEM),
        compiler_params=PARAMS,
        name="project",
    )(weight, arrived)


def block_kernel(*refs):
    *projected, side, act, terms, terms_out = refs
    hidden, rows = act.shape
    groups = side.shape[1] // rows
    part = hidden // groups
    if len(projected) == 2:
        nodes = (projected[0][...] + projected[1][...].astype(jnp.float32)).astype(jnp.bfloat16)
    else:
        nodes = projected[0][...]
    adjacency = side[:rows, :]
    preact = dot(nodes, adjacency, 1, 1)
    normal_cdf = 0.5 * (1.0 + lax.erf(preact * root_half))
    normal_pdf = jnp.exp(-0.5 * preact * preact) * inv_root_two_pi
    act[...] = (preact * normal_cdf).astype(act.dtype)
    derivative = normal_cdf + preact * normal_pdf
    cotangent = jnp.concatenate(
        [side[rows : rows + part, group * rows : (group + 1) * rows] for group in range(groups)], 0
    )
    pre_grad = (cotangent.astype(jnp.float32) * derivative).astype(jnp.bfloat16)
    value = dot(pre_grad, adjacency, 1, 0)
    terms[...] = value
    terms_out[...] = value.astype(terms_out.dtype)


def block(projected, side, rows):
    hidden, cluster = projected[0].shape
    return pl.pallas_call(
        block_kernel,
        out_shape=(
            jax.ShapeDtypeStruct((hidden, rows), jnp.bfloat16),
            jax.ShapeDtypeStruct((hidden, cluster), jnp.float32),
            jax.ShapeDtypeStruct((hidden, cluster), jnp.bfloat16),
        ),
        in_specs=[VMEM] * (len(projected) + 1),
        out_specs=(VMEM,) * 3,
        compiler_params=PARAMS,
        name="block",
    )(*projected, side)


def gradient_kernel(arrived, part, other, terms, held, sems):
    places, columns, width, rows = arrived.shape
    count = held.shape[0]
    size = columns // count
    node_grad = (part[...] + other[...].astype(jnp.float32)).astype(jnp.bfloat16)
    copies = []
    for group in range(count):
        total = None
        for place in range(places):
            nodes = arrived[place, group * size : (group + 1) * size].reshape(size * width, rows)
            value = dot(nodes, node_grad[:, place * rows : (place + 1) * rows], 1, 1)
            total = value if total is None else total + value
        if len(terms.shape) == 2:
            held[group] = total
            target = terms.at[pl.ds(group * size * width, size * width)]
        else:
            share = terms.shape[2]
            total = total.astype(terms.dtype).reshape(size, places, share, total.shape[1])
            for place in range(places):
                held[group, place] = total[:, place]
            target = terms.at[:, pl.ds(group * size, size)]
        copies.append(pltpu.make_async_copy(held.at[group], target, sems.at[group]))
        copies[-1].start()
    for copy in copies:
        copy.wait()


def gradient(arrived, part, other, shape, dtype):
    count = 2
    if len(shape) == 2:
        held = (count, shape[0] // count, shape[1])
    else:
        held = (count, shape[0], shape[1] // count) + shape[2:]
    return pl.pallas_call(
        gradient_kernel,
        out_shape=jax.ShapeDtypeStruct(shape, dtype),
        in_specs=[VMEM] * 3,
        out_specs=ANY,
        scratch_shapes=[pltpu.VMEM(held, dtype), pltpu.SemaphoreType.DMA((count,))],
        compiler_params=PARAMS,
        name="gradient",
    )(arrived, part, other)


def finish_kernel(terms, act, total_out, act_out, total, sems):
    act_copy = pltpu.make_async_copy(act, act_out, sems.at[0])
    act_copy.start()
    total[...] = jnp.sum(terms[...].astype(jnp.float32), axis=0)
    total_copy = pltpu.make_async_copy(total, total_out, sems.at[1])
    total_copy.start()
    act_copy.wait()
    total_copy.wait()


def finish(terms, act):
    return pl.pallas_call(
        finish_kernel,
        out_shape=(
            jax.ShapeDtypeStruct(terms.shape[1:], jnp.float32),
            jax.ShapeDtypeStruct(act.shape, act.dtype),
        ),
        in_specs=[VMEM, ANY],
        out_specs=(ANY, ANY),
        scratch_shapes=[
            pltpu.VMEM(terms.shape[1:], jnp.float32),
            pltpu.SemaphoreType.DMA((2,)),
        ],
        compiler_params=PARAMS,
        name="finish",
    )(terms, act)


def per_device(feats, weight, tile_row, tile_col, tile_block, tile_count, edge_blocks, cotangent):
    columns = lax.axis_size("col")
    pairs = lax.axis_size("hi")
    core = lax.axis_index("core")
    width, shard_nodes = feats.shape
    rows = shard_nodes // (2 * columns)
    hidden = weight.shape[1]
    bf16 = jnp.bfloat16

    chunks = by_destination(feats, 2, columns).reshape(2 * columns, width, rows)
    arrived = lax.all_to_all(chunks, ("lo", "col"), split_axis=0, concat_axis=0, tiled=True)
    arrived = arrived.reshape(2, columns, width, rows)

    side = side_inputs(
        tile_row[0, 0], tile_col[0, 0], tile_block[0, 0], tile_count[0], edge_blocks[0, 0], cotangent
    )
    side = lax.ppermute(side, ("core", "lo"), TRANSPOSE)
    own_weight = lax.dynamic_index_in_dim(
        weight.reshape(columns, 2, width, hidden), core, 1, keepdims=False
    ).reshape(columns * width, hidden).T
    arrived, side, own_weight = lax.optimization_barrier((arrived, side, own_weight))

    part, sent = project(own_weight, arrived)
    other = lax.ppermute(sent, "core", SWAP)
    projected = (part, other)
    if pairs > 1:
        total = (part + other.astype(jnp.float32)).astype(bf16)
        projected = (lax.all_gather(total, "hi", axis=1, tiled=True),)
    output, part, sent = block(projected, side, rows)
    if pairs > 1:
        part = lax.psum_scatter(part, "hi", scatter_dimension=1, tiled=True)
        sent = part.astype(bf16)
    other = lax.ppermute(sent, "core", SWAP)
    act = lax.ppermute(output, ("core", "lo"), TRANSPOSE)
    share = width // (2 * pairs)
    if pairs > 1:
        terms = gradient(arrived, part, other, (columns * width, hidden), jnp.float32)
        terms = terms.reshape(columns, pairs, 2, share, hidden)
        terms = lax.psum_scatter(terms, "hi", scatter_dimension=1, tiled=True).astype(bf16)
        terms = terms[:, 0].transpose(1, 0, 2, 3)
    else:
        terms = gradient(arrived, part, other, (2, columns, share, hidden), bf16)
    terms = terms.reshape(2 * columns, share, hidden)
    terms = lax.all_to_all(terms, ("lo", "col"), split_axis=0, concat_axis=0, tiled=True)
    weight_grad, act = finish(terms, act)
    return (act, weight_grad)


def solution(mesh):
    n_feat, n_node = mesh.shape["feat"], mesh.shape["node"]
    fine = Mesh(
        mesh.devices.reshape(n_feat // 2, 2, n_node // 2, 2), ("col", "core", "hi", "lo")
    )
    feat, node = ("col", "core"), ("hi", "lo")
    return jax.shard_map(
        per_device,
        mesh=fine,
        in_specs=(
            P(feat, node),
            P(),
            P(feat, node, None),
            P(feat, node, None),
            P(feat, node, None),
            P(feat, node),
            P(feat, node, None, None, None),
            P(None, node + feat),
        ),
        out_specs=(P(None, node + feat), P(feat + node, None)),
        check_vma=False,
    )
```

```python
import functools

import jax
import jax.numpy as jnp
from jax import lax
from jax.experimental import pallas as pl
from jax.experimental.pallas import tpu as pltpu
from jax.sharding import Mesh, PartitionSpec as P

root_half = 0.7071067811865476
inv_root_two_pi = 0.3989422804014327

SWAP = ((0, 1), (1, 0))
TRANSPOSE = ((0, 0), (1, 2), (2, 1), (3, 3))
VMEM = pl.BlockSpec(memory_space=pltpu.VMEM)
SMEM = pl.BlockSpec(memory_space=pltpu.SMEM)
ANY = pl.BlockSpec(memory_space=pl.ANY)
PARAMS = pltpu.CompilerParams(vmem_limit_bytes=24 * 1024 * 1024)


def middle_first(columns):
    return sorted(range(columns), key=lambda column: abs(2 * column - columns - 1))


def dot(left, right, left_dim, right_dim):
    return lax.dot_general(
        left, right, (((left_dim,), (right_dim,)), ((), ())), preferred_element_type=jnp.float32
    )


def chunk_kernel(feats, chunks, held, in_sems, out_sems):
    places, columns, _, rows = chunks.shape
    rank = {column: at for at, column in enumerate(middle_first(columns))}
    spots = [
        (places - 1 - place, rank[column]) for column in range(columns) for place in range(places)
    ]
    loads, stores = [], []
    for at, (place, column) in enumerate(spots):
        loads.append(
            pltpu.make_async_copy(
                feats.at[:, pl.ds(at * rows, rows)], held.at[place, column], in_sems.at[at]
            )
        )
        stores.append(
            pltpu.make_async_copy(held.at[place, column], chunks.at[place, column], out_sems.at[at])
        )
    for load in loads:
        load.start()
    for load, store in zip(loads, stores):
        load.wait()
        store.start()
    for store in stores:
        store.wait()


def by_destination(feats, places, columns):
    width, nodes = feats.shape
    shape = (places, columns, width, nodes // (places * columns))
    return pl.pallas_call(
        chunk_kernel,
        out_shape=jax.ShapeDtypeStruct(shape, feats.dtype),
        in_specs=[pl.BlockSpec(memory_space=pltpu.HBM)],
        out_specs=pl.BlockSpec(memory_space=pltpu.HBM),
        scratch_shapes=[
            pltpu.VMEM(shape, feats.dtype),
            pltpu.SemaphoreType.DMA((places * columns,)),
            pltpu.SemaphoreType.DMA((places * columns,)),
        ],
        compiler_params=pltpu.CompilerParams(vmem_limit_bytes=60 * 1024 * 1024),
        name="by_destination",
    )(feats)


def side_kernel(row_tile, col_tile, block_index, live, blocks, cotangent, out):
    slots, tile, _ = blocks.shape
    hidden, rows = cotangent.shape
    groups = out.shape[1] // rows
    part = hidden // groups
    for slot in range(slots):
        row = pl.multiple_of(row_tile[slot] * tile, tile)
        col = pl.multiple_of(col_tile[slot] * tile, tile)
        block = blocks[block_index[slot]]
        out[pl.ds(row, tile), pl.ds(col, tile)] = jnp.where(
            slot < live[0], block, jnp.zeros_like(block)
        )
    for group in range(groups):
        out[rows : rows + part, group * rows : (group + 1) * rows] = cotangent[
            group * part : (group + 1) * part, :
        ]


def side_inputs(row_tile, col_tile, block_index, live, blocks, cotangent):
    slots, tile, _ = blocks.shape
    hidden, rows = cotangent.shape
    cluster = slots * tile * tile // rows
    return pl.pallas_call(
        side_kernel,
        out_shape=jax.ShapeDtypeStruct((rows + hidden * rows // cluster, cluster), blocks.dtype),
        in_specs=[SMEM] * 4 + [VMEM] * 2,
        out_specs=VMEM,
        compiler_params=PARAMS,
        name="side_inputs",
    )(row_tile, col_tile, block_index, live, blocks, cotangent)


def project_kernel(weight, arrived, part, part_out):
    places, columns, width, rows = arrived.shape
    for place in range(places):
        nodes = arrived[places - 1 - place].reshape(columns * width, rows)
        value = dot(weight[...], nodes, 1, 0)
        part[:, place * rows : (place + 1) * rows] = value
        part_out[:, place * rows : (place + 1) * rows] = value.astype(part_out.dtype)


def project(weight, arrived):
    hidden = weight.shape[0]
    places, columns, width, rows = arrived.shape
    shape = (hidden, places * rows)
    return pl.pallas_call(
        project_kernel,
        out_shape=(
            jax.ShapeDtypeStruct(shape, jnp.float32),
            jax.ShapeDtypeStruct(shape, jnp.bfloat16),
        ),
        in_specs=[VMEM, VMEM],
        out_specs=(VMEM, VMEM),
        compiler_params=PARAMS,
        name="project",
    )(weight, arrived)


def parts(side, rows, hidden):
    groups = side.shape[1] // rows
    part = hidden // groups
    cotangent = jnp.concatenate(
        [side[rows : rows + part, group * rows : (group + 1) * rows] for group in range(groups)], 0
    )
    return side[:rows, :], cotangent


def block_terms(nodes, side, rows, act=None):
    adjacency, cotangent = parts(side, rows, nodes.shape[0])
    preact = dot(nodes, adjacency, 1, 1)
    normal_cdf = 0.5 * (1.0 + lax.erf(preact * root_half))
    normal_pdf = jnp.exp(-0.5 * preact * preact) * inv_root_two_pi
    if act is not None:
        act[...] = (preact * normal_cdf).astype(act.dtype)
    derivative = normal_cdf + preact * normal_pdf
    pre_grad = (cotangent.astype(jnp.float32) * derivative).astype(jnp.bfloat16)
    return dot(pre_grad, adjacency, 1, 0)


def gradient_terms(arrived, node_grad, terms, held, sems):
    places, columns, width, rows = arrived.shape
    count = held.shape[0]
    size = columns // count
    copies = []
    for group in range(count):
        total = None
        for place in range(places):
            source = places - 1 - place
            nodes = arrived[source, group * size : (group + 1) * size].reshape(size * width, rows)
            value = dot(nodes, node_grad[:, place * rows : (place + 1) * rows], 1, 1)
            total = value if total is None else total + value
        if len(terms.shape) == 2:
            held[group] = total
            target = terms.at[pl.ds(group * size * width, size * width)]
        else:
            share = terms.shape[2]
            total = total.astype(terms.dtype).reshape(size, places, share, total.shape[1])
            for place in range(places):
                held[group, places - 1 - place] = total[:, place]
            target = terms.at[:, pl.ds(group * size, size)]
        copies.append(pltpu.make_async_copy(held.at[group], target, sems.at[group]))
        copies[-1].start()
    for copy in copies:
        copy.wait()


def own_kernel(part, other, side, act, nodes, total):
    nodes[...] = (part[...] + other[...].astype(jnp.float32)).astype(nodes.dtype)
    total[...] = block_terms(nodes[...], side, act.shape[1], act)


def pair_kernel(nodes, side, own_total, arrived, terms, held, sems):
    rows = arrived.shape[3]
    total = own_total[...] + block_terms(nodes[...], side, rows)
    gradient_terms(arrived, total.astype(jnp.bfloat16), terms, held, sems)


def node_kernel(nodes, own, pair, act, total):
    rows = act.shape[1]
    total[...] = block_terms(nodes[...], own, rows, act) + block_terms(nodes[...], pair, rows)


def gradient_kernel(arrived, node_grad, terms, held, sems):
    gradient_terms(arrived, node_grad[...], terms, held, sems)


def gradient_scratch(shape, dtype):
    count = 2
    if len(shape) == 2:
        held = (count, shape[0] // count, shape[1])
    else:
        held = (count, shape[0], shape[1] // count) + shape[2:]
    return [pltpu.VMEM(held, dtype), pltpu.SemaphoreType.DMA((count,))]


def own_block(part, other, side, rows):
    hidden, cluster = part.shape
    return pl.pallas_call(
        own_kernel,
        out_shape=(
            jax.ShapeDtypeStruct((hidden, rows), jnp.bfloat16),
            jax.ShapeDtypeStruct((hidden, cluster), jnp.bfloat16),
            jax.ShapeDtypeStruct((hidden, cluster), jnp.float32),
        ),
        in_specs=[VMEM] * 3,
        out_specs=(VMEM,) * 3,
        compiler_params=PARAMS,
        name="own_block",
    )(part, other, side)


def pair_block(nodes, side, own_total, arrived, shape):
    return pl.pallas_call(
        pair_kernel,
        out_shape=jax.ShapeDtypeStruct(shape, jnp.bfloat16),
        in_specs=[VMEM] * 4,
        out_specs=ANY,
        scratch_shapes=gradient_scratch(shape, jnp.bfloat16),
        compiler_params=PARAMS,
        name="pair_block",
    )(nodes, side, own_total, arrived)


def node_sums(nodes, own, pair, rows):
    act = jax.ShapeDtypeStruct((nodes.shape[0], rows), jnp.bfloat16)
    return pl.pallas_call(
        node_kernel,
        out_shape=(act, jax.ShapeDtypeStruct(nodes.shape, jnp.float32)),
        in_specs=[VMEM] * 3,
        out_specs=(VMEM, VMEM),
        compiler_params=PARAMS,
        name="block",
    )(nodes, own, pair)


def gradient(arrived, node_grad, shape):
    return pl.pallas_call(
        gradient_kernel,
        out_shape=jax.ShapeDtypeStruct(shape, jnp.float32),
        in_specs=[VMEM] * 2,
        out_specs=ANY,
        scratch_shapes=gradient_scratch(shape, jnp.float32),
        compiler_params=PARAMS,
        name="gradient",
    )(arrived, node_grad)


def finish_kernel(terms, act, total_out, act_out, total, sems):
    act_copy = pltpu.make_async_copy(act, act_out, sems.at[0])
    act_copy.start()
    total[...] = jnp.sum(terms[...].astype(jnp.float32), axis=0)
    total_copy = pltpu.make_async_copy(total, total_out, sems.at[1])
    total_copy.start()
    act_copy.wait()
    total_copy.wait()


def finish(terms, act):
    return pl.pallas_call(
        finish_kernel,
        out_shape=(
            jax.ShapeDtypeStruct(terms.shape[1:], jnp.float32),
            jax.ShapeDtypeStruct(act.shape, act.dtype),
        ),
        in_specs=[VMEM, ANY],
        out_specs=(ANY, ANY),
        scratch_shapes=[
            pltpu.VMEM(terms.shape[1:], jnp.float32),
            pltpu.SemaphoreType.DMA((2,)),
        ],
        compiler_params=PARAMS,
        name="finish",
    )(terms, act)


def per_device(feats, weight, tile_row, tile_col, tile_block, tile_count, edge_blocks, cotangent):
    columns = lax.axis_size("col")
    pairs = lax.axis_size("hi")
    core = lax.axis_index("core")
    width, shard_nodes = feats.shape
    rows = shard_nodes // (2 * columns)
    hidden = weight.shape[1]
    bf16 = jnp.bfloat16
    order = middle_first(columns)
    axes = ("col", "core", "hi", "lo")
    groups = [
        [((column * 2 + c) * pairs + hi) * 2 + place for place in (1, 0) for column in order]
        for c in range(2)
        for hi in range(pairs)
    ]

    chunks = by_destination(feats, 2, columns).reshape(2 * columns, width, rows)
    arrived = lax.all_to_all(
        chunks, axes, split_axis=0, concat_axis=0, tiled=True, axis_index_groups=groups
    )
    arrived = arrived.reshape(2, columns, width, rows)

    side = side_inputs(
        tile_row[0, 0], tile_col[0, 0], tile_block[0, 0], tile_count[0], edge_blocks[0, 0], cotangent
    )
    side = lax.ppermute(side, ("core", "lo"), TRANSPOSE)
    own_weight = lax.dynamic_index_in_dim(
        weight.reshape(columns, 2, width, hidden), core, 1, keepdims=False
    )
    own_weight = jnp.stack([own_weight[column] for column in order])
    own_weight = own_weight.reshape(columns * width, hidden).T
    arrived, side, own_weight = lax.optimization_barrier((arrived, side, own_weight))
    side_pair = lax.ppermute(side, "core", SWAP)

    part, sent = project(own_weight, arrived)
    other = lax.ppermute(sent, "core", SWAP)
    share = width // (2 * pairs)
    if pairs > 1:
        nodes = (part + other.astype(jnp.float32)).astype(bf16)
        nodes = lax.all_gather(nodes, "hi", axis=1, tiled=True)
        output, node_grad = node_sums(nodes, side, side_pair, rows)
        node_grad = lax.psum_scatter(node_grad, "hi", scatter_dimension=1, tiled=True)
        terms = gradient(arrived, node_grad.astype(bf16), (columns * width, hidden))
        terms = terms.reshape(columns, pairs, 2, share, hidden)
        terms = lax.psum_scatter(terms, "hi", scatter_dimension=1, tiled=True).astype(bf16)
        terms = terms[:, 0, ::-1].transpose(1, 0, 2, 3)
    else:
        output, nodes, total = own_block(part, other, side, rows)
        terms = pair_block(nodes, side_pair, total, arrived, (2, columns, share, hidden))
    act = lax.ppermute(output, ("core", "lo"), TRANSPOSE)
    terms = terms.reshape(2 * columns, share, hidden)
    terms = lax.all_to_all(
        terms, axes, split_axis=0, concat_axis=0, tiled=True, axis_index_groups=groups
    )
    weight_grad, act = finish(terms, act)
    return (act, weight_grad)


def solution(mesh):
    n_feat, n_node = mesh.shape["feat"], mesh.shape["node"]
    fine = Mesh(
        mesh.devices.reshape(n_feat // 2, 2, n_node // 2, 2), ("col", "core", "hi", "lo")
    )
    feat, node = ("col", "core"), ("hi", "lo")
    return jax.shard_map(
        per_device,
        mesh=fine,
        in_specs=(
            P(feat, node),
            P(),
            P(feat, node, None),
            P(feat, node, None),
            P(feat, node, None),
            P(feat, node),
            P(feat, node, None, None, None),
            P(None, node + feat),
        ),
        out_specs=(P(None, node + feat), P(feat + node, None)),
        check_vma=False,
    )
```

```python
import functools

import jax
import jax.numpy as jnp
from jax import lax
from jax.experimental import pallas as pl
from jax.experimental.pallas import tpu as pltpu
from jax.sharding import Mesh, PartitionSpec as P

root_half = 0.7071067811865476
inv_root_two_pi = 0.3989422804014327

SWAP = ((0, 1), (1, 0))
TRANSPOSE = ((0, 0), (1, 2), (2, 1), (3, 3))
VMEM = pl.BlockSpec(memory_space=pltpu.VMEM)
SMEM = pl.BlockSpec(memory_space=pltpu.SMEM)
ANY = pl.BlockSpec(memory_space=pl.ANY)
PARAMS = pltpu.CompilerParams(vmem_limit_bytes=24 * 1024 * 1024)


def middle_first(columns):
    quarter = columns // 4
    order = [at * quarter + rest for at in (2, 1, 3, 0) for rest in reversed(range(quarter))]
    order.remove(columns // 2)
    return [columns // 2] + order


def dot(left, right, left_dim, right_dim):
    return lax.dot_general(
        left, right, (((left_dim,), (right_dim,)), ((), ())), preferred_element_type=jnp.float32
    )


def chunk_kernel(feats, chunks, held, in_sems, out_sems):
    places, columns, _, rows = chunks.shape
    rank = {column: at for at, column in enumerate(middle_first(columns))}
    spots = [
        (places - 1 - place, rank[column]) for column in range(columns) for place in range(places)
    ]
    loads, stores = [], []
    for at, (place, column) in enumerate(spots):
        loads.append(
            pltpu.make_async_copy(
                feats.at[:, pl.ds(at * rows, rows)], held.at[place, column], in_sems.at[at]
            )
        )
        stores.append(
            pltpu.make_async_copy(held.at[place, column], chunks.at[place, column], out_sems.at[at])
        )
    for load in loads:
        load.start()
    for load, store in zip(loads, stores):
        load.wait()
        store.start()
    for store in stores:
        store.wait()


def by_destination(feats, places, columns):
    width, nodes = feats.shape
    shape = (places, columns, width, nodes // (places * columns))
    return pl.pallas_call(
        chunk_kernel,
        out_shape=jax.ShapeDtypeStruct(shape, feats.dtype),
        in_specs=[pl.BlockSpec(memory_space=pltpu.HBM)],
        out_specs=pl.BlockSpec(memory_space=pltpu.HBM),
        scratch_shapes=[
            pltpu.VMEM(shape, feats.dtype),
            pltpu.SemaphoreType.DMA((places * columns,)),
            pltpu.SemaphoreType.DMA((places * columns,)),
        ],
        compiler_params=pltpu.CompilerParams(vmem_limit_bytes=60 * 1024 * 1024),
        name="by_destination",
    )(feats)


def side_kernel(row_tile, col_tile, block_index, live, blocks, cotangent, out):
    slots, tile, _ = blocks.shape
    hidden, rows = cotangent.shape
    groups = out.shape[1] // rows
    part = hidden // groups
    for slot in range(slots):
        row = pl.multiple_of(row_tile[slot] * tile, tile)
        col = pl.multiple_of(col_tile[slot] * tile, tile)
        block = blocks[block_index[slot]]
        out[pl.ds(row, tile), pl.ds(col, tile)] = jnp.where(
            slot < live[0], block, jnp.zeros_like(block)
        )
    for group in range(groups):
        out[rows : rows + part, group * rows : (group + 1) * rows] = cotangent[
            group * part : (group + 1) * part, :
        ]


def side_inputs(row_tile, col_tile, block_index, live, blocks, cotangent):
    slots, tile, _ = blocks.shape
    hidden, rows = cotangent.shape
    cluster = slots * tile * tile // rows
    return pl.pallas_call(
        side_kernel,
        out_shape=jax.ShapeDtypeStruct((rows + hidden * rows // cluster, cluster), blocks.dtype),
        in_specs=[SMEM] * 4 + [VMEM] * 2,
        out_specs=VMEM,
        compiler_params=PARAMS,
        name="side_inputs",
    )(row_tile, col_tile, block_index, live, blocks, cotangent)


def project_kernel(weight, arrived, part, part_out):
    places, columns, width, rows = arrived.shape
    for place in range(places):
        nodes = arrived[places - 1 - place].reshape(columns * width, rows)
        value = dot(weight[...], nodes, 1, 0)
        part[:, place * rows : (place + 1) * rows] = value
        part_out[:, place * rows : (place + 1) * rows] = value.astype(part_out.dtype)


def project(weight, arrived):
    hidden = weight.shape[0]
    places, columns, width, rows = arrived.shape
    shape = (hidden, places * rows)
    return pl.pallas_call(
        project_kernel,
        out_shape=(
            jax.ShapeDtypeStruct(shape, jnp.float32),
            jax.ShapeDtypeStruct(shape, jnp.bfloat16),
        ),
        in_specs=[VMEM, VMEM],
        out_specs=(VMEM, VMEM),
        compiler_params=PARAMS,
        name="project",
    )(weight, arrived)


def parts(side, rows, hidden):
    groups = side.shape[1] // rows
    part = hidden // groups
    cotangent = jnp.concatenate(
        [side[rows : rows + part, group * rows : (group + 1) * rows] for group in range(groups)], 0
    )
    return side[:rows, :], cotangent


def block_terms(nodes, side, rows, act=None):
    adjacency, cotangent = parts(side, rows, nodes.shape[0])
    preact = dot(nodes, adjacency, 1, 1)
    normal_cdf = 0.5 * (1.0 + lax.erf(preact * root_half))
    normal_pdf = jnp.exp(-0.5 * preact * preact) * inv_root_two_pi
    if act is not None:
        act[...] = (preact * normal_cdf).astype(act.dtype)
    derivative = normal_cdf + preact * normal_pdf
    pre_grad = (cotangent.astype(jnp.float32) * derivative).astype(jnp.bfloat16)
    return dot(pre_grad, adjacency, 1, 0)


def gradient_terms(arrived, node_grad, terms, held, sems):
    places, columns, width, rows = arrived.shape
    count = held.shape[0]
    size = columns // count
    copies = []
    for group in range(count):
        total = None
        for place in range(places):
            source = places - 1 - place
            nodes = arrived[source, group * size : (group + 1) * size].reshape(size * width, rows)
            value = dot(nodes, node_grad[:, place * rows : (place + 1) * rows], 1, 1)
            total = value if total is None else total + value
        if len(terms.shape) == 2:
            held[group] = total
            target = terms.at[pl.ds(group * size * width, size * width)]
        else:
            share = terms.shape[2]
            total = total.astype(terms.dtype).reshape(size, places, share, total.shape[1])
            for place in range(places):
                held[group, places - 1 - place] = total[:, place]
            target = terms.at[:, pl.ds(group * size, size)]
        copies.append(pltpu.make_async_copy(held.at[group], target, sems.at[group]))
        copies[-1].start()
    for copy in copies:
        copy.wait()


def whole_kernel(part, other, own, pair, arrived, act, terms, held, sems):
    rows = act.shape[1]
    nodes = (part[...] + other[...].astype(jnp.float32)).astype(jnp.bfloat16)
    total = block_terms(nodes, own, rows, act) + block_terms(nodes, pair, rows)
    gradient_terms(arrived, total.astype(jnp.bfloat16), terms, held, sems)


def node_kernel(nodes, own, pair, act, total):
    rows = act.shape[1]
    total[...] = block_terms(nodes[...], own, rows, act) + block_terms(nodes[...], pair, rows)


def gradient_kernel(arrived, node_grad, terms, held, sems):
    gradient_terms(arrived, node_grad[...], terms, held, sems)


def gradient_scratch(shape, dtype):
    count = 2
    if len(shape) == 2:
        held = (count, shape[0] // count, shape[1])
    else:
        held = (count, shape[0], shape[1] // count) + shape[2:]
    return [pltpu.VMEM(held, dtype), pltpu.SemaphoreType.DMA((count,))]


def whole(part, other, own, pair, arrived, rows, shape):
    act = jax.ShapeDtypeStruct((part.shape[0], rows), jnp.bfloat16)
    return pl.pallas_call(
        whole_kernel,
        out_shape=(act, jax.ShapeDtypeStruct(shape, jnp.bfloat16)),
        in_specs=[VMEM] * 5,
        out_specs=(VMEM, ANY),
        scratch_shapes=gradient_scratch(shape, jnp.bfloat16),
        compiler_params=PARAMS,
        name="blocks_and_gradient",
    )(part, other, own, pair, arrived)


def node_sums(nodes, own, pair, rows):
    act = jax.ShapeDtypeStruct((nodes.shape[0], rows), jnp.bfloat16)
    return pl.pallas_call(
        node_kernel,
        out_shape=(act, jax.ShapeDtypeStruct(nodes.shape, jnp.float32)),
        in_specs=[VMEM] * 3,
        out_specs=(VMEM, VMEM),
        compiler_params=PARAMS,
        name="block",
    )(nodes, own, pair)


def gradient(arrived, node_grad, shape):
    return pl.pallas_call(
        gradient_kernel,
        out_shape=jax.ShapeDtypeStruct(shape, jnp.float32),
        in_specs=[VMEM] * 2,
        out_specs=ANY,
        scratch_shapes=gradient_scratch(shape, jnp.float32),
        compiler_params=PARAMS,
        name="gradient",
    )(arrived, node_grad)


def finish_kernel(terms, act, total_out, act_out, total, sems):
    act_copy = pltpu.make_async_copy(act, act_out, sems.at[0])
    act_copy.start()
    total[...] = jnp.sum(terms[...].astype(jnp.float32), axis=0)
    total_copy = pltpu.make_async_copy(total, total_out, sems.at[1])
    total_copy.start()
    act_copy.wait()
    total_copy.wait()


def finish(terms, act):
    return pl.pallas_call(
        finish_kernel,
        out_shape=(
            jax.ShapeDtypeStruct(terms.shape[1:], jnp.float32),
            jax.ShapeDtypeStruct(act.shape, act.dtype),
        ),
        in_specs=[VMEM, ANY],
        out_specs=(ANY, ANY),
        scratch_shapes=[
            pltpu.VMEM(terms.shape[1:], jnp.float32),
            pltpu.SemaphoreType.DMA((2,)),
        ],
        compiler_params=PARAMS,
        name="finish",
    )(terms, act)


def per_device(feats, weight, tile_row, tile_col, tile_block, tile_count, edge_blocks, cotangent):
    columns = lax.axis_size("col")
    pairs = lax.axis_size("hi")
    core = lax.axis_index("core")
    width, shard_nodes = feats.shape
    rows = shard_nodes // (2 * columns)
    hidden = weight.shape[1]
    bf16 = jnp.bfloat16
    order = middle_first(columns)
    axes = ("col", "core", "hi", "lo")
    groups = [
        [((column * 2 + c) * pairs + hi) * 2 + place for place in (1, 0) for column in order]
        for c in range(2)
        for hi in range(pairs)
    ]

    chunks = by_destination(feats, 2, columns).reshape(2 * columns, width, rows)
    arrived = lax.all_to_all(
        chunks, axes, split_axis=0, concat_axis=0, tiled=True, axis_index_groups=groups
    )
    arrived = arrived.reshape(2, columns, width, rows)

    side = side_inputs(
        tile_row[0, 0], tile_col[0, 0], tile_block[0, 0], tile_count[0], edge_blocks[0, 0], cotangent
    )
    side = lax.ppermute(side, ("core", "lo"), TRANSPOSE)
    own_weight = lax.dynamic_index_in_dim(
        weight.reshape(columns, 2, width, hidden), core, 1, keepdims=False
    )
    own_weight = jnp.stack([own_weight[column] for column in order])
    own_weight = own_weight.reshape(columns * width, hidden).T
    arrived, side, own_weight = lax.optimization_barrier((arrived, side, own_weight))
    side_pair = lax.ppermute(side, "core", SWAP)

    part, sent = project(own_weight, arrived)
    other = lax.ppermute(sent, "core", SWAP)
    share = width // (2 * pairs)
    if pairs > 1:
        nodes = (part + other.astype(jnp.float32)).astype(bf16)
        nodes = lax.all_gather(nodes, "hi", axis=1, tiled=True)
        output, node_grad = node_sums(nodes, side, side_pair, rows)
        node_grad = lax.psum_scatter(node_grad, "hi", scatter_dimension=1, tiled=True)
        terms = gradient(arrived, node_grad.astype(bf16), (columns * width, hidden))
        terms = terms.reshape(columns, pairs, 2, share, hidden)
        terms = lax.psum_scatter(terms, "hi", scatter_dimension=1, tiled=True).astype(bf16)
        terms = terms[:, 0, ::-1].transpose(1, 0, 2, 3)
    else:
        output, terms = whole(
            part, other, side, side_pair, arrived, rows, (2, columns, share, hidden)
        )
    act = lax.ppermute(output, ("core", "lo"), TRANSPOSE)
    terms = terms.reshape(2 * columns, share, hidden)
    terms = lax.all_to_all(
        terms, axes, split_axis=0, concat_axis=0, tiled=True, axis_index_groups=groups
    )
    weight_grad, act = finish(terms, act)
    return (act, weight_grad)


def solution(mesh):
    n_feat, n_node = mesh.shape["feat"], mesh.shape["node"]
    fine = Mesh(
        mesh.devices.reshape(n_feat // 2, 2, n_node // 2, 2), ("col", "core", "hi", "lo")
    )
    feat, node = ("col", "core"), ("hi", "lo")
    return jax.shard_map(
        per_device,
        mesh=fine,
        in_specs=(
            P(feat, node),
            P(),
            P(feat, node, None),
            P(feat, node, None),
            P(feat, node, None),
            P(feat, node),
            P(feat, node, None, None, None),
            P(None, node + feat),
        ),
        out_specs=(P(None, node + feat), P(feat + node, None)),
        check_vma=False,
    )
```

```python
import functools

import jax
import jax.numpy as jnp
from jax import lax
from jax.experimental import pallas as pl
from jax.experimental.pallas import tpu as pltpu
from jax.sharding import Mesh, PartitionSpec as P

root_half = 0.7071067811865476
inv_root_two_pi = 0.3989422804014327

SWAP = ((0, 1), (1, 0))
TRANSPOSE = ((0, 0), (1, 2), (2, 1), (3, 3))
VMEM = pl.BlockSpec(memory_space=pltpu.VMEM)
SMEM = pl.BlockSpec(memory_space=pltpu.SMEM)
ANY = pl.BlockSpec(memory_space=pl.ANY)
PARAMS = pltpu.CompilerParams(vmem_limit_bytes=24 * 1024 * 1024)


def middle_first(columns):
    quarter = max(columns // 4, 1)
    rest = sorted(range(columns), key=lambda column: -column)
    order = [column for at in (2, 1, 3, 0) for column in rest if min(column // quarter, 3) == at]
    order.remove(columns // 2)
    return [columns // 2] + order


def dot(left, right, left_dim, right_dim):
    return lax.dot_general(
        left, right, (((left_dim,), (right_dim,)), ((), ())), preferred_element_type=jnp.float32
    )


def chunk_kernel(feats, chunks, held, in_sems, out_sems):
    places, columns, _, rows = chunks.shape
    for place in range(places):
        for at, column in enumerate(middle_first(columns)):
            source = (column * places + places - 1 - place) * rows
            pltpu.make_async_copy(
                feats.at[:, pl.ds(source, rows)], held.at[place, at], in_sems.at[place]
            ).start()
    stores = []
    for place in range(places):
        pltpu.make_async_copy(held.at[place], held.at[place], in_sems.at[place]).wait()
        stores.append(
            pltpu.make_async_copy(held.at[place], chunks.at[place], out_sems.at[place])
        )
        stores[-1].start()
    for store in stores:
        store.wait()


def by_destination(feats, places, columns):
    width, nodes = feats.shape
    shape = (places, columns, width, nodes // (places * columns))
    return pl.pallas_call(
        chunk_kernel,
        out_shape=jax.ShapeDtypeStruct(shape, feats.dtype),
        in_specs=[pl.BlockSpec(memory_space=pltpu.HBM)],
        out_specs=pl.BlockSpec(memory_space=pltpu.HBM),
        scratch_shapes=[
            pltpu.VMEM(shape, feats.dtype),
            pltpu.SemaphoreType.DMA((places,)),
            pltpu.SemaphoreType.DMA((places,)),
        ],
        compiler_params=pltpu.CompilerParams(vmem_limit_bytes=60 * 1024 * 1024),
        name="by_destination",
    )(feats)


def side_kernel(row_tile, col_tile, block_index, live, blocks, cotangent, out):
    slots, tile, _ = blocks.shape
    hidden, rows = cotangent.shape
    groups = out.shape[1] // rows
    part = hidden // groups
    for slot in range(slots):
        row = pl.multiple_of(row_tile[slot] * tile, tile)
        col = pl.multiple_of(col_tile[slot] * tile, tile)
        block = blocks[block_index[slot]]
        out[pl.ds(row, tile), pl.ds(col, tile)] = jnp.where(
            slot < live[0], block, jnp.zeros_like(block)
        )
    for group in range(groups):
        out[rows : rows + part, group * rows : (group + 1) * rows] = cotangent[
            group * part : (group + 1) * part, :
        ]


def side_inputs(row_tile, col_tile, block_index, live, blocks, cotangent):
    slots, tile, _ = blocks.shape
    hidden, rows = cotangent.shape
    cluster = slots * tile * tile // rows
    return pl.pallas_call(
        side_kernel,
        out_shape=jax.ShapeDtypeStruct((rows + hidden * rows // cluster, cluster), blocks.dtype),
        in_specs=[SMEM] * 4 + [VMEM] * 2,
        out_specs=VMEM,
        compiler_params=PARAMS,
        name="side_inputs",
    )(row_tile, col_tile, block_index, live, blocks, cotangent)


def project_kernel(weight, arrived, part, part_out):
    places, columns, width, rows = arrived.shape
    for place in range(places):
        nodes = arrived[places - 1 - place].reshape(columns * width, rows)
        value = dot(weight[...], nodes, 1, 0)
        part[:, place * rows : (place + 1) * rows] = value
        part_out[:, place * rows : (place + 1) * rows] = value.astype(part_out.dtype)


def project(weight, arrived):
    hidden = weight.shape[0]
    places, columns, width, rows = arrived.shape
    shape = (hidden, places * rows)
    return pl.pallas_call(
        project_kernel,
        out_shape=(
            jax.ShapeDtypeStruct(shape, jnp.float32),
            jax.ShapeDtypeStruct(shape, jnp.bfloat16),
        ),
        in_specs=[VMEM, VMEM],
        out_specs=(VMEM, VMEM),
        compiler_params=PARAMS,
        name="project",
    )(weight, arrived)


def parts(side, rows, hidden):
    groups = side.shape[1] // rows
    part = hidden // groups
    cotangent = jnp.concatenate(
        [side[rows : rows + part, group * rows : (group + 1) * rows] for group in range(groups)], 0
    )
    return side[:rows, :], cotangent


def block_terms(nodes, side, rows, act=None):
    adjacency, cotangent = parts(side, rows, nodes.shape[0])
    preact = dot(nodes, adjacency, 1, 1)
    normal_cdf = 0.5 * (1.0 + lax.erf(preact * root_half))
    normal_pdf = jnp.exp(-0.5 * preact * preact) * inv_root_two_pi
    if act is not None:
        act[...] = (preact * normal_cdf).astype(act.dtype)
    derivative = normal_cdf + preact * normal_pdf
    pre_grad = (cotangent.astype(jnp.float32) * derivative).astype(jnp.bfloat16)
    return dot(pre_grad, adjacency, 1, 0)


def gradient_terms(arrived, node_grad, terms, held, sems):
    places, columns, width, rows = arrived.shape
    count = held.shape[0]
    size = columns // count
    copies = []
    for group in range(count):
        total = None
        for place in range(places):
            source = places - 1 - place
            nodes = arrived[source, group * size : (group + 1) * size].reshape(size * width, rows)
            value = dot(nodes, node_grad[:, place * rows : (place + 1) * rows], 1, 1)
            total = value if total is None else total + value
        if len(terms.shape) == 2:
            held[group] = total
            target = terms.at[pl.ds(group * size * width, size * width)]
        else:
            share = terms.shape[2]
            total = total.astype(terms.dtype).reshape(size, places, share, total.shape[1])
            for place in range(places):
                held[group, places - 1 - place] = total[:, place]
            target = terms.at[:, pl.ds(group * size, size)]
        copies.append(pltpu.make_async_copy(held.at[group], target, sems.at[group]))
        copies[-1].start()
    for copy in copies:
        copy.wait()


def whole_kernel(part, other, own, pair, arrived, act, terms, held, sems):
    rows = act.shape[1]
    nodes = (part[...] + other[...].astype(jnp.float32)).astype(jnp.bfloat16)
    total = block_terms(nodes, own, rows, act) + block_terms(nodes, pair, rows)
    gradient_terms(arrived, total.astype(jnp.bfloat16), terms, held, sems)


def node_kernel(nodes, own, pair, act, total):
    rows = act.shape[1]
    total[...] = block_terms(nodes[...], own, rows, act) + block_terms(nodes[...], pair, rows)


def gradient_kernel(arrived, node_grad, terms, held, sems):
    gradient_terms(arrived, node_grad[...], terms, held, sems)


def gradient_scratch(shape, dtype):
    count = 2
    if len(shape) == 2:
        held = (count, shape[0] // count, shape[1])
    else:
        held = (count, shape[0], shape[1] // count) + shape[2:]
    return [pltpu.VMEM(held, dtype), pltpu.SemaphoreType.DMA((count,))]


def whole(part, other, own, pair, arrived, rows, shape):
    act = jax.ShapeDtypeStruct((part.shape[0], rows), jnp.bfloat16)
    return pl.pallas_call(
        whole_kernel,
        out_shape=(act, jax.ShapeDtypeStruct(shape, jnp.bfloat16)),
        in_specs=[VMEM] * 5,
        out_specs=(VMEM, ANY),
        scratch_shapes=gradient_scratch(shape, jnp.bfloat16),
        compiler_params=PARAMS,
        name="blocks_and_gradient",
    )(part, other, own, pair, arrived)


def node_sums(nodes, own, pair, rows):
    act = jax.ShapeDtypeStruct((nodes.shape[0], rows), jnp.bfloat16)
    return pl.pallas_call(
        node_kernel,
        out_shape=(act, jax.ShapeDtypeStruct(nodes.shape, jnp.float32)),
        in_specs=[VMEM] * 3,
        out_specs=(VMEM, VMEM),
        compiler_params=PARAMS,
        name="block",
    )(nodes, own, pair)


def gradient(arrived, node_grad, shape):
    return pl.pallas_call(
        gradient_kernel,
        out_shape=jax.ShapeDtypeStruct(shape, jnp.float32),
        in_specs=[VMEM] * 2,
        out_specs=ANY,
        scratch_shapes=gradient_scratch(shape, jnp.float32),
        compiler_params=PARAMS,
        name="gradient",
    )(arrived, node_grad)


def finish_kernel(terms, act, total_out, act_out, total, sems):
    act_copy = pltpu.make_async_copy(act, act_out, sems.at[0])
    act_copy.start()
    total[...] = jnp.sum(terms[...].astype(jnp.float32), axis=0)
    total_copy = pltpu.make_async_copy(total, total_out, sems.at[1])
    total_copy.start()
    act_copy.wait()
    total_copy.wait()


def finish(terms, act):
    return pl.pallas_call(
        finish_kernel,
        out_shape=(
            jax.ShapeDtypeStruct(terms.shape[1:], jnp.float32),
            jax.ShapeDtypeStruct(act.shape, act.dtype),
        ),
        in_specs=[VMEM, ANY],
        out_specs=(ANY, ANY),
        scratch_shapes=[
            pltpu.VMEM(terms.shape[1:], jnp.float32),
            pltpu.SemaphoreType.DMA((2,)),
        ],
        compiler_params=PARAMS,
        name="finish",
    )(terms, act)


def per_device(feats, weight, tile_row, tile_col, tile_block, tile_count, edge_blocks, cotangent):
    columns = lax.axis_size("col")
    pairs = lax.axis_size("hi")
    core = lax.axis_index("core")
    width, shard_nodes = feats.shape
    rows = shard_nodes // (2 * columns)
    hidden = weight.shape[1]
    bf16 = jnp.bfloat16
    order = middle_first(columns)
    axes = ("col", "core", "hi", "lo")
    groups = [
        [((column * 2 + c) * pairs + hi) * 2 + place for place in (1, 0) for column in order]
        for c in range(2)
        for hi in range(pairs)
    ]

    chunks = by_destination(feats, 2, columns).reshape(2 * columns, width, rows)
    arrived = lax.all_to_all(
        chunks, axes, split_axis=0, concat_axis=0, tiled=True, axis_index_groups=groups
    )
    arrived = arrived.reshape(2, columns, width, rows)

    side = side_inputs(
        tile_row[0, 0], tile_col[0, 0], tile_block[0, 0], tile_count[0], edge_blocks[0, 0], cotangent
    )
    side = lax.ppermute(side, ("core", "lo"), TRANSPOSE)
    own_weight = lax.dynamic_index_in_dim(
        weight.reshape(columns, 2, width, hidden), core, 1, keepdims=False
    )
    own_weight = jnp.stack([own_weight[column] for column in order])
    own_weight = own_weight.reshape(columns * width, hidden).T
    arrived, side, own_weight = lax.optimization_barrier((arrived, side, own_weight))
    side_pair = lax.ppermute(side, "core", SWAP)

    part, sent = project(own_weight, arrived)
    other = lax.ppermute(sent, "core", SWAP)
    share = width // (2 * pairs)
    if pairs > 1:
        nodes = (part + other.astype(jnp.float32)).astype(bf16)
        nodes = lax.all_gather(nodes, "hi", axis=1, tiled=True)
        output, node_grad = node_sums(nodes, side, side_pair, rows)
        node_grad = lax.psum_scatter(node_grad, "hi", scatter_dimension=1, tiled=True)
        terms = gradient(arrived, node_grad.astype(bf16), (columns * width, hidden))
        terms = terms.reshape(columns, pairs, 2, share, hidden)
        terms = lax.psum_scatter(terms, "hi", scatter_dimension=1, tiled=True).astype(bf16)
        terms = terms[:, 0, ::-1].transpose(1, 0, 2, 3)
    else:
        output, terms = whole(
            part, other, side, side_pair, arrived, rows, (2, columns, share, hidden)
        )
    act = lax.ppermute(output, ("core", "lo"), TRANSPOSE)
    terms = terms.reshape(2 * columns, share, hidden)
    terms = lax.all_to_all(
        terms, axes, split_axis=0, concat_axis=0, tiled=True, axis_index_groups=groups
    )
    weight_grad, act = finish(terms, act)
    return (act, weight_grad)


def solution(mesh):
    n_feat, n_node = mesh.shape["feat"], mesh.shape["node"]
    fine = Mesh(
        mesh.devices.reshape(n_feat // 2, 2, n_node // 2, 2), ("col", "core", "hi", "lo")
    )
    feat, node = ("col", "core"), ("hi", "lo")
    return jax.shard_map(
        per_device,
        mesh=fine,
        in_specs=(
            P(feat, node),
            P(),
            P(feat, node, None),
            P(feat, node, None),
            P(feat, node, None),
            P(feat, node),
            P(feat, node, None, None, None),
            P(None, node + feat),
        ),
        out_specs=(P(None, node + feat), P(feat + node, None)),
        check_vma=False,
    )
```

```python
import functools

import jax
import jax.numpy as jnp
from jax import lax
from jax.experimental import pallas as pl
from jax.experimental.pallas import tpu as pltpu
from jax.sharding import Mesh, PartitionSpec as P

root_half = 0.7071067811865476
inv_root_two_pi = 0.3989422804014327

SWAP = ((0, 1), (1, 0))
TRANSPOSE = ((0, 0), (1, 2), (2, 1), (3, 3))
VMEM = pl.BlockSpec(memory_space=pltpu.VMEM)
SMEM = pl.BlockSpec(memory_space=pltpu.SMEM)
ANY = pl.BlockSpec(memory_space=pl.ANY)
PARAMS = pltpu.CompilerParams(vmem_limit_bytes=24 * 1024 * 1024)


def middle_first(columns):
    quarter = max(columns // 4, 1)
    rest = sorted(range(columns), key=lambda column: -column)
    order = [column for at in (2, 1, 3, 0) for column in rest if min(column // quarter, 3) == at]
    order.remove(columns // 2)
    return [columns // 2] + order


def dot(left, right, left_dim, right_dim):
    return lax.dot_general(
        left, right, (((left_dim,), (right_dim,)), ((), ())), preferred_element_type=jnp.float32
    )


def chunk_kernel(feats, chunks, held, in_sems, out_sems):
    places, columns, _, rows = chunks.shape
    for place in range(places):
        for at, column in enumerate(middle_first(columns)):
            source = (column * places + places - 1 - place) * rows
            pltpu.make_async_copy(
                feats.at[:, pl.ds(source, rows)], held.at[place, at], in_sems.at[place]
            ).start()
    stores = []
    for place in range(places):
        pltpu.make_async_copy(held.at[place], held.at[place], in_sems.at[place]).wait()
        stores.append(
            pltpu.make_async_copy(held.at[place], chunks.at[place], out_sems.at[place])
        )
        stores[-1].start()
    for store in stores:
        store.wait()


def by_destination(feats, places, columns):
    width, nodes = feats.shape
    shape = (places, columns, width, nodes // (places * columns))
    return pl.pallas_call(
        chunk_kernel,
        out_shape=jax.ShapeDtypeStruct(shape, feats.dtype),
        in_specs=[pl.BlockSpec(memory_space=pltpu.HBM)],
        out_specs=pl.BlockSpec(memory_space=pltpu.HBM),
        scratch_shapes=[
            pltpu.VMEM(shape, feats.dtype),
            pltpu.SemaphoreType.DMA((places,)),
            pltpu.SemaphoreType.DMA((places,)),
        ],
        compiler_params=pltpu.CompilerParams(vmem_limit_bytes=60 * 1024 * 1024),
        name="by_destination",
    )(feats)


def side_kernel(row_tile, col_tile, block_index, live, blocks, cotangent, out):
    slots, tile, _ = blocks.shape
    hidden, rows = cotangent.shape
    groups = out.shape[1] // rows
    part = hidden // groups
    for slot in range(slots):
        row = pl.multiple_of(row_tile[slot] * tile, tile)
        col = pl.multiple_of(col_tile[slot] * tile, tile)
        block = blocks[block_index[slot]]
        out[pl.ds(row, tile), pl.ds(col, tile)] = jnp.where(
            slot < live[0], block, jnp.zeros_like(block)
        )
    for group in range(groups):
        out[rows : rows + part, group * rows : (group + 1) * rows] = cotangent[
            group * part : (group + 1) * part, :
        ]


def side_inputs(row_tile, col_tile, block_index, live, blocks, cotangent):
    slots, tile, _ = blocks.shape
    hidden, rows = cotangent.shape
    cluster = slots * tile * tile // rows
    return pl.pallas_call(
        side_kernel,
        out_shape=jax.ShapeDtypeStruct((rows + hidden * rows // cluster, cluster), blocks.dtype),
        in_specs=[SMEM] * 4 + [VMEM] * 2,
        out_specs=VMEM,
        compiler_params=PARAMS,
        name="side_inputs",
    )(row_tile, col_tile, block_index, live, blocks, cotangent)


def project_kernel(weight, arrived, part, part_out):
    places, columns, width, rows = arrived.shape
    for place in range(places):
        nodes = arrived[places - 1 - place].reshape(columns * width, rows)
        value = dot(weight[...], nodes, 1, 0)
        part[:, place * rows : (place + 1) * rows] = value
        part_out[:, place * rows : (place + 1) * rows] = value.astype(part_out.dtype)


def project(weight, arrived):
    hidden = weight.shape[0]
    places, columns, width, rows = arrived.shape
    shape = (hidden, places * rows)
    return pl.pallas_call(
        project_kernel,
        out_shape=(
            jax.ShapeDtypeStruct(shape, jnp.float32),
            jax.ShapeDtypeStruct(shape, jnp.bfloat16),
        ),
        in_specs=[VMEM, VMEM],
        out_specs=(VMEM, VMEM),
        compiler_params=PARAMS,
        name="project",
    )(weight, arrived)


def parts(side, rows, hidden):
    groups = side.shape[1] // rows
    part = hidden // groups
    cotangent = jnp.concatenate(
        [side[rows : rows + part, group * rows : (group + 1) * rows] for group in range(groups)], 0
    )
    return side[:rows, :], cotangent


def block_grads(nodes, side, rows, act=None):
    adjacency, cotangent = parts(side, rows, nodes.shape[0])
    preact = dot(nodes, adjacency, 1, 1)
    normal_cdf = 0.5 * (1.0 + lax.erf(preact * root_half))
    normal_pdf = jnp.exp(-0.5 * preact * preact) * inv_root_two_pi
    if act is not None:
        act[...] = (preact * normal_cdf).astype(act.dtype)
    derivative = normal_cdf + preact * normal_pdf
    return (cotangent.astype(jnp.float32) * derivative).astype(jnp.bfloat16)


def block_terms(nodes, side, rows, act=None):
    return dot(block_grads(nodes, side, rows, act), side[:rows, :], 1, 0)


def spread_kernel(arrived, *refs):
    *sides, out = refs
    places, columns, width, rows = arrived.shape
    for at, side in enumerate(sides):
        total = None
        for place in range(places):
            nodes = arrived[places - 1 - place].reshape(columns * width, rows)
            value = dot(nodes, side[:rows, place * rows : (place + 1) * rows], 1, 1)
            total = value if total is None else total + value
        out[:, at * rows : (at + 1) * rows] = total.astype(out.dtype)


def spread(arrived, sides):
    _, columns, width, rows = arrived.shape
    shape = (columns * width, len(sides) * rows)
    return pl.pallas_call(
        spread_kernel,
        out_shape=jax.ShapeDtypeStruct(shape, arrived.dtype),
        in_specs=[VMEM] * (1 + len(sides)),
        out_specs=VMEM,
        compiler_params=PARAMS,
        cost_estimate=pl.CostEstimate(
            flops=4 * shape[0] * shape[1] * rows, bytes_accessed=4 * shape[0] * shape[1], transcendentals=0
        ),
        name="spread",
    )(arrived, *sides)


def gradient_terms(arrived, node_grad, terms, held, sems):
    places, columns, width, rows = arrived.shape
    count = held.shape[0]
    size = columns // count
    copies = []
    for group in range(count):
        total = None
        for place in range(places):
            source = places - 1 - place
            nodes = arrived[source, group * size : (group + 1) * size].reshape(size * width, rows)
            value = dot(nodes, node_grad[:, place * rows : (place + 1) * rows], 1, 1)
            total = value if total is None else total + value
        if len(terms.shape) == 2:
            held[group] = total
            target = terms.at[pl.ds(group * size * width, size * width)]
        else:
            share = terms.shape[2]
            total = total.astype(terms.dtype).reshape(size, places, share, total.shape[1])
            for place in range(places):
                held[group, places - 1 - place] = total[:, place]
            target = terms.at[:, pl.ds(group * size, size)]
        copies.append(pltpu.make_async_copy(held.at[group], target, sems.at[group]))
        copies[-1].start()
    for copy in copies:
        copy.wait()


def whole_kernel(part, other, own, pair, hidden, act, terms, held, sems):
    rows = act.shape[1]
    nodes = (part[...] + other[...].astype(jnp.float32)).astype(jnp.bfloat16)
    grads = [block_grads(nodes, own, rows, act), block_grads(nodes, pair, rows)]
    count, places, size, share, units = held.shape
    height = hidden.shape[0] // count
    copies = []
    for group in range(count):
        taken = hidden[group * height : (group + 1) * height, :]
        total = dot(taken[:, :rows], grads[0], 1, 1) + dot(taken[:, rows:], grads[1], 1, 1)
        total = total.astype(terms.dtype).reshape(size, places, share, units)
        for place in range(places):
            held[group, places - 1 - place] = total[:, place]
        target = terms.at[:, pl.ds(group * size, size)]
        copies.append(pltpu.make_async_copy(held.at[group], target, sems.at[group]))
        copies[-1].start()
    for copy in copies:
        copy.wait()


def node_kernel(nodes, own, pair, act, total):
    rows = act.shape[1]
    total[...] = block_terms(nodes[...], own, rows, act) + block_terms(nodes[...], pair, rows)


def gradient_kernel(arrived, node_grad, terms, held, sems):
    gradient_terms(arrived, node_grad[...], terms, held, sems)


def gradient_scratch(shape, dtype):
    count = 2
    if len(shape) == 2:
        held = (count, shape[0] // count, shape[1])
    else:
        held = (count, shape[0], shape[1] // count) + shape[2:]
    return [pltpu.VMEM(held, dtype), pltpu.SemaphoreType.DMA((count,))]


def whole(part, other, own, pair, hidden, rows, shape):
    act = jax.ShapeDtypeStruct((part.shape[0], rows), jnp.bfloat16)
    return pl.pallas_call(
        whole_kernel,
        out_shape=(act, jax.ShapeDtypeStruct(shape, jnp.bfloat16)),
        in_specs=[VMEM] * 5,
        out_specs=(VMEM, ANY),
        scratch_shapes=gradient_scratch(shape, jnp.bfloat16),
        compiler_params=PARAMS,
        name="blocks_and_gradient",
    )(part, other, own, pair, hidden)


def node_sums(nodes, own, pair, rows):
    act = jax.ShapeDtypeStruct((nodes.shape[0], rows), jnp.bfloat16)
    return pl.pallas_call(
        node_kernel,
        out_shape=(act, jax.ShapeDtypeStruct(nodes.shape, jnp.float32)),
        in_specs=[VMEM] * 3,
        out_specs=(VMEM, VMEM),
        compiler_params=PARAMS,
        name="block",
    )(nodes, own, pair)


def gradient(arrived, node_grad, shape):
    return pl.pallas_call(
        gradient_kernel,
        out_shape=jax.ShapeDtypeStruct(shape, jnp.float32),
        in_specs=[VMEM] * 2,
        out_specs=ANY,
        scratch_shapes=gradient_scratch(shape, jnp.float32),
        compiler_params=PARAMS,
        name="gradient",
    )(arrived, node_grad)


def finish_kernel(terms, act, total_out, act_out, total, sems):
    act_copy = pltpu.make_async_copy(act, act_out, sems.at[0])
    act_copy.start()
    total[...] = jnp.sum(terms[...].astype(jnp.float32), axis=0)
    total_copy = pltpu.make_async_copy(total, total_out, sems.at[1])
    total_copy.start()
    act_copy.wait()
    total_copy.wait()


def finish(terms, act):
    return pl.pallas_call(
        finish_kernel,
        out_shape=(
            jax.ShapeDtypeStruct(terms.shape[1:], jnp.float32),
            jax.ShapeDtypeStruct(act.shape, act.dtype),
        ),
        in_specs=[VMEM, ANY],
        out_specs=(ANY, ANY),
        scratch_shapes=[
            pltpu.VMEM(terms.shape[1:], jnp.float32),
            pltpu.SemaphoreType.DMA((2,)),
        ],
        compiler_params=PARAMS,
        name="finish",
    )(terms, act)


def per_device(feats, weight, tile_row, tile_col, tile_block, tile_count, edge_blocks, cotangent):
    columns = lax.axis_size("col")
    pairs = lax.axis_size("hi")
    core = lax.axis_index("core")
    width, shard_nodes = feats.shape
    rows = shard_nodes // (2 * columns)
    hidden = weight.shape[1]
    bf16 = jnp.bfloat16
    order = middle_first(columns)
    axes = ("col", "core", "hi", "lo")
    groups = [
        [((column * 2 + c) * pairs + hi) * 2 + place for place in (1, 0) for column in order]
        for c in range(2)
        for hi in range(pairs)
    ]

    chunks = by_destination(feats, 2, columns).reshape(2 * columns, width, rows)
    arrived = lax.all_to_all(
        chunks, axes, split_axis=0, concat_axis=0, tiled=True, axis_index_groups=groups
    )
    arrived = arrived.reshape(2, columns, width, rows)

    side = side_inputs(
        tile_row[0, 0], tile_col[0, 0], tile_block[0, 0], tile_count[0], edge_blocks[0, 0], cotangent
    )
    side = lax.ppermute(side, ("core", "lo"), TRANSPOSE)
    own_weight = lax.dynamic_index_in_dim(
        weight.reshape(columns, 2, width, hidden), core, 1, keepdims=False
    )
    own_weight = jnp.stack([own_weight[column] for column in order])
    own_weight = own_weight.reshape(columns * width, hidden).T
    arrived, side, own_weight = lax.optimization_barrier((arrived, side, own_weight))
    side_pair = lax.ppermute(side, "core", SWAP)

    part, sent = project(own_weight, arrived)
    sent, arrived = lax.optimization_barrier((sent, arrived))
    other = lax.ppermute(sent, "core", SWAP)
    share = width // (2 * pairs)
    if pairs > 1:
        nodes = (part + other.astype(jnp.float32)).astype(bf16)
        nodes = lax.all_gather(nodes, "hi", axis=1, tiled=True)
        output, node_grad = node_sums(nodes, side, side_pair, rows)
        node_grad = lax.psum_scatter(node_grad, "hi", scatter_dimension=1, tiled=True)
        terms = gradient(arrived, node_grad.astype(bf16), (columns * width, hidden))
        terms = terms.reshape(columns, pairs, 2, share, hidden)
        terms = lax.psum_scatter(terms, "hi", scatter_dimension=1, tiled=True).astype(bf16)
        terms = terms[:, 0, ::-1].transpose(1, 0, 2, 3)
    else:
        summed = spread(arrived, (side, side_pair))
        output, terms = whole(
            part, other, side, side_pair, summed, rows, (2, columns, share, hidden)
        )
    act = lax.ppermute(output, ("core", "lo"), TRANSPOSE)
    terms = terms.reshape(2 * columns, share, hidden)
    terms = lax.all_to_all(
        terms, axes, split_axis=0, concat_axis=0, tiled=True, axis_index_groups=groups
    )
    weight_grad, act = finish(terms, act)
    return (act, weight_grad)


def solution(mesh):
    n_feat, n_node = mesh.shape["feat"], mesh.shape["node"]
    fine = Mesh(
        mesh.devices.reshape(n_feat // 2, 2, n_node // 2, 2), ("col", "core", "hi", "lo")
    )
    feat, node = ("col", "core"), ("hi", "lo")
    return jax.shard_map(
        per_device,
        mesh=fine,
        in_specs=(
            P(feat, node),
            P(),
            P(feat, node, None),
            P(feat, node, None),
            P(feat, node, None),
            P(feat, node),
            P(feat, node, None, None, None),
            P(None, node + feat),
        ),
        out_specs=(P(None, node + feat), P(feat + node, None)),
        check_vma=False,
    )
```

```python
import functools

import jax
import jax.numpy as jnp
from jax import lax
from jax.experimental import pallas as pl
from jax.experimental.pallas import tpu as pltpu
from jax.sharding import Mesh, PartitionSpec as P

root_half = 0.7071067811865476
inv_root_two_pi = 0.3989422804014327

SWAP = ((0, 1), (1, 0))
TRANSPOSE = ((0, 0), (1, 2), (2, 1), (3, 3))
VMEM = pl.BlockSpec(memory_space=pltpu.VMEM)
SMEM = pl.BlockSpec(memory_space=pltpu.SMEM)
ANY = pl.BlockSpec(memory_space=pl.ANY)
PARAMS = pltpu.CompilerParams(vmem_limit_bytes=24 * 1024 * 1024)


def middle_first(columns, quarters=(2, 1, 0, 3)):
    quarter = max(columns // 4, 1)
    rest = sorted(range(columns), key=lambda column: -column)
    order = [column for at in quarters for column in rest if min(column // quarter, 3) == at]
    order.remove(columns // 2)
    return [columns // 2] + order


SECOND = (2, 1, 3, 0)


def dot(left, right, left_dim, right_dim):
    return lax.dot_general(
        left, right, (((left_dim,), (right_dim,)), ((), ())), preferred_element_type=jnp.float32
    )


def chunk_kernel(feats, chunks, held, in_sems, out_sems):
    places, columns, _, rows = chunks.shape
    for place in range(places):
        for at, column in enumerate(middle_first(columns)):
            source = (column * places + places - 1 - place) * rows
            pltpu.make_async_copy(
                feats.at[:, pl.ds(source, rows)], held.at[place, at], in_sems.at[place]
            ).start()
    stores = []
    for place in range(places):
        pltpu.make_async_copy(held.at[place], held.at[place], in_sems.at[place]).wait()
        stores.append(
            pltpu.make_async_copy(held.at[place], chunks.at[place], out_sems.at[place])
        )
        stores[-1].start()
    for store in stores:
        store.wait()


def by_destination(feats, places, columns):
    width, nodes = feats.shape
    shape = (places, columns, width, nodes // (places * columns))
    return pl.pallas_call(
        chunk_kernel,
        out_shape=jax.ShapeDtypeStruct(shape, feats.dtype),
        in_specs=[pl.BlockSpec(memory_space=pltpu.HBM)],
        out_specs=pl.BlockSpec(memory_space=pltpu.HBM),
        scratch_shapes=[
            pltpu.VMEM(shape, feats.dtype),
            pltpu.SemaphoreType.DMA((places,)),
            pltpu.SemaphoreType.DMA((places,)),
        ],
        compiler_params=pltpu.CompilerParams(vmem_limit_bytes=60 * 1024 * 1024),
        name="by_destination",
    )(feats)


def side_kernel(row_tile, col_tile, block_index, live, blocks, cotangent, out):
    slots, tile, _ = blocks.shape
    hidden, rows = cotangent.shape
    groups = out.shape[1] // rows
    part = hidden // groups
    for slot in range(slots):
        row = pl.multiple_of(row_tile[slot] * tile, tile)
        col = pl.multiple_of(col_tile[slot] * tile, tile)
        block = blocks[block_index[slot]]
        out[pl.ds(row, tile), pl.ds(col, tile)] = jnp.where(
            slot < live[0], block, jnp.zeros_like(block)
        )
    for group in range(groups):
        out[rows : rows + part, group * rows : (group + 1) * rows] = cotangent[
            group * part : (group + 1) * part, :
        ]


def side_inputs(row_tile, col_tile, block_index, live, blocks, cotangent):
    slots, tile, _ = blocks.shape
    hidden, rows = cotangent.shape
    cluster = slots * tile * tile // rows
    return pl.pallas_call(
        side_kernel,
        out_shape=jax.ShapeDtypeStruct((rows + hidden * rows // cluster, cluster), blocks.dtype),
        in_specs=[SMEM] * 4 + [VMEM] * 2,
        out_specs=VMEM,
        compiler_params=PARAMS,
        name="side_inputs",
    )(row_tile, col_tile, block_index, live, blocks, cotangent)


def project_kernel(weight, arrived, part, part_out):
    places, columns, width, rows = arrived.shape
    for place in range(places):
        nodes = arrived[places - 1 - place].reshape(columns * width, rows)
        value = dot(weight[...], nodes, 1, 0)
        part[:, place * rows : (place + 1) * rows] = value
        part_out[:, place * rows : (place + 1) * rows] = value.astype(part_out.dtype)


def project(weight, arrived):
    hidden = weight.shape[0]
    places, columns, width, rows = arrived.shape
    shape = (hidden, places * rows)
    return pl.pallas_call(
        project_kernel,
        out_shape=(
            jax.ShapeDtypeStruct(shape, jnp.float32),
            jax.ShapeDtypeStruct(shape, jnp.bfloat16),
        ),
        in_specs=[VMEM, VMEM],
        out_specs=(VMEM, VMEM),
        compiler_params=PARAMS,
        name="project",
    )(weight, arrived)


def parts(side, rows, hidden):
    groups = side.shape[1] // rows
    part = hidden // groups
    cotangent = jnp.concatenate(
        [side[rows : rows + part, group * rows : (group + 1) * rows] for group in range(groups)], 0
    )
    return side[:rows, :], cotangent


def block_grads(nodes, side, rows, act=None):
    adjacency, cotangent = parts(side, rows, nodes.shape[0])
    preact = dot(nodes, adjacency, 1, 1)
    normal_cdf = 0.5 * (1.0 + lax.erf(preact * root_half))
    normal_pdf = jnp.exp(-0.5 * preact * preact) * inv_root_two_pi
    if act is not None:
        act[...] = (preact * normal_cdf).astype(act.dtype)
    derivative = normal_cdf + preact * normal_pdf
    return (cotangent.astype(jnp.float32) * derivative).astype(jnp.bfloat16)


def block_terms(nodes, side, rows, act=None):
    return dot(block_grads(nodes, side, rows, act), side[:rows, :], 1, 0)


def spread_kernel(arrived, *refs):
    *sides, out = refs
    places, columns, width, rows = arrived.shape
    for at, side in enumerate(sides):
        total = None
        for place in range(places):
            nodes = arrived[places - 1 - place].reshape(columns * width, rows)
            value = dot(nodes, side[:rows, place * rows : (place + 1) * rows], 1, 1)
            total = value if total is None else total + value
        out[:, at * rows : (at + 1) * rows] = total.astype(out.dtype)


def spread(arrived, sides):
    _, columns, width, rows = arrived.shape
    shape = (columns * width, len(sides) * rows)
    return pl.pallas_call(
        spread_kernel,
        out_shape=jax.ShapeDtypeStruct(shape, arrived.dtype),
        in_specs=[VMEM] * (1 + len(sides)),
        out_specs=VMEM,
        compiler_params=PARAMS,
        cost_estimate=pl.CostEstimate(
            flops=4 * shape[0] * shape[1] * rows, bytes_accessed=4 * shape[0] * shape[1], transcendentals=0
        ),
        name="spread",
    )(arrived, *sides)


def gradient_terms(arrived, node_grad, terms, held, sems):
    places, columns, width, rows = arrived.shape
    count = held.shape[0]
    size = columns // count
    copies = []
    for group in range(count):
        total = None
        for place in range(places):
            source = places - 1 - place
            nodes = arrived[source, group * size : (group + 1) * size].reshape(size * width, rows)
            value = dot(nodes, node_grad[:, place * rows : (place + 1) * rows], 1, 1)
            total = value if total is None else total + value
        if len(terms.shape) == 2:
            held[group] = total
            target = terms.at[pl.ds(group * size * width, size * width)]
        else:
            share = terms.shape[2]
            total = total.astype(terms.dtype).reshape(size, places, share, total.shape[1])
            for place in range(places):
                held[group, places - 1 - place] = total[:, place]
            target = terms.at[:, pl.ds(group * size, size)]
        copies.append(pltpu.make_async_copy(held.at[group], target, sems.at[group]))
        copies[-1].start()
    for copy in copies:
        copy.wait()


def whole_kernel(part, other, own, pair, hidden, act, terms, held, sem):
    rows = act.shape[1]
    nodes = (part[...] + other[...].astype(jnp.float32)).astype(jnp.bfloat16)
    grads = [block_grads(nodes, own, rows, act), block_grads(nodes, pair, rows)]
    places, columns, share, units = held.shape
    count = 2
    size = columns // count
    order = middle_first(columns)
    rank = {column: at for at, column in enumerate(middle_first(columns, SECOND))}
    height = hidden.shape[0] // count
    for group in range(count):
        taken = hidden[group * height : (group + 1) * height, :]
        total = dot(taken[:, :rows], grads[0], 1, 1) + dot(taken[:, rows:], grads[1], 1, 1)
        total = total.astype(terms.dtype).reshape(size, places, share, units)
        for at in range(size):
            for place in range(places):
                held[places - 1 - place, rank[order[group * size + at]]] = total[at, place]
    copy = pltpu.make_async_copy(held, terms, sem)
    copy.start()
    copy.wait()


def node_kernel(nodes, own, pair, act, total):
    rows = act.shape[1]
    total[...] = block_terms(nodes[...], own, rows, act) + block_terms(nodes[...], pair, rows)


def gradient_kernel(arrived, node_grad, terms, held, sems):
    gradient_terms(arrived, node_grad[...], terms, held, sems)


def gradient_scratch(shape, dtype):
    count = 2
    if len(shape) == 2:
        held = (count, shape[0] // count, shape[1])
    else:
        held = (count, shape[0], shape[1] // count) + shape[2:]
    return [pltpu.VMEM(held, dtype), pltpu.SemaphoreType.DMA((count,))]


def whole(part, other, own, pair, hidden, rows, shape):
    act = jax.ShapeDtypeStruct((part.shape[0], rows), jnp.bfloat16)
    return pl.pallas_call(
        whole_kernel,
        out_shape=(act, jax.ShapeDtypeStruct(shape, jnp.bfloat16)),
        in_specs=[VMEM] * 5,
        out_specs=(VMEM, ANY),
        scratch_shapes=[pltpu.VMEM(shape, jnp.bfloat16), pltpu.SemaphoreType.DMA],
        compiler_params=PARAMS,
        name="blocks_and_gradient",
    )(part, other, own, pair, hidden)


def node_sums(nodes, own, pair, rows):
    act = jax.ShapeDtypeStruct((nodes.shape[0], rows), jnp.bfloat16)
    return pl.pallas_call(
        node_kernel,
        out_shape=(act, jax.ShapeDtypeStruct(nodes.shape, jnp.float32)),
        in_specs=[VMEM] * 3,
        out_specs=(VMEM, VMEM),
        compiler_params=PARAMS,
        name="block",
    )(nodes, own, pair)


def gradient(arrived, node_grad, shape):
    return pl.pallas_call(
        gradient_kernel,
        out_shape=jax.ShapeDtypeStruct(shape, jnp.float32),
        in_specs=[VMEM] * 2,
        out_specs=ANY,
        scratch_shapes=gradient_scratch(shape, jnp.float32),
        compiler_params=PARAMS,
        name="gradient",
    )(arrived, node_grad)


def finish_kernel(terms, act, total_out, act_out, total, sems):
    act_copy = pltpu.make_async_copy(act, act_out, sems.at[0])
    act_copy.start()
    total[...] = jnp.sum(terms[...].astype(jnp.float32), axis=0)
    total_copy = pltpu.make_async_copy(total, total_out, sems.at[1])
    total_copy.start()
    act_copy.wait()
    total_copy.wait()


def finish(terms, act):
    return pl.pallas_call(
        finish_kernel,
        out_shape=(
            jax.ShapeDtypeStruct(terms.shape[1:], jnp.float32),
            jax.ShapeDtypeStruct(act.shape, act.dtype),
        ),
        in_specs=[VMEM, ANY],
        out_specs=(ANY, ANY),
        scratch_shapes=[
            pltpu.VMEM(terms.shape[1:], jnp.float32),
            pltpu.SemaphoreType.DMA((2,)),
        ],
        compiler_params=PARAMS,
        name="finish",
    )(terms, act)


def per_device(feats, weight, tile_row, tile_col, tile_block, tile_count, edge_blocks, cotangent):
    columns = lax.axis_size("col")
    pairs = lax.axis_size("hi")
    core = lax.axis_index("core")
    width, shard_nodes = feats.shape
    rows = shard_nodes // (2 * columns)
    hidden = weight.shape[1]
    bf16 = jnp.bfloat16
    order = middle_first(columns)
    axes = ("col", "core", "hi", "lo")

    def groups(listed):
        return [
            [((column * 2 + c) * pairs + hi) * 2 + place for place in (1, 0) for column in listed]
            for c in range(2)
            for hi in range(pairs)
        ]

    second = middle_first(columns, SECOND)

    chunks = by_destination(feats, 2, columns).reshape(2 * columns, width, rows)
    arrived = lax.all_to_all(
        chunks, axes, split_axis=0, concat_axis=0, tiled=True, axis_index_groups=groups(order)
    )
    arrived = arrived.reshape(2, columns, width, rows)

    side = side_inputs(
        tile_row[0, 0], tile_col[0, 0], tile_block[0, 0], tile_count[0], edge_blocks[0, 0], cotangent
    )
    side = lax.ppermute(side, ("core", "lo"), TRANSPOSE)
    own_weight = lax.dynamic_index_in_dim(
        weight.reshape(columns, 2, width, hidden), core, 1, keepdims=False
    )
    own_weight = jnp.stack([own_weight[column] for column in order])
    own_weight = own_weight.reshape(columns * width, hidden).T
    arrived, side, own_weight = lax.optimization_barrier((arrived, side, own_weight))
    side_pair = lax.ppermute(side, "core", SWAP)

    part, sent = project(own_weight, arrived)
    sent, arrived = lax.optimization_barrier((sent, arrived))
    other = lax.ppermute(sent, "core", SWAP)
    share = width // (2 * pairs)
    if pairs > 1:
        nodes = (part + other.astype(jnp.float32)).astype(bf16)
        nodes = lax.all_gather(nodes, "hi", axis=1, tiled=True)
        output, node_grad = node_sums(nodes, side, side_pair, rows)
        node_grad = lax.psum_scatter(node_grad, "hi", scatter_dimension=1, tiled=True)
        terms = gradient(arrived, node_grad.astype(bf16), (columns * width, hidden))
        terms = terms.reshape(columns, pairs, 2, share, hidden)
        terms = lax.psum_scatter(terms, "hi", scatter_dimension=1, tiled=True).astype(bf16)
        terms = jnp.stack([terms[order.index(column), 0, ::-1] for column in second], 1)
    else:
        summed = spread(arrived, (side, side_pair))
        output, terms = whole(
            part, other, side, side_pair, summed, rows, (2, columns, share, hidden)
        )
    act = lax.ppermute(output, ("core", "lo"), TRANSPOSE)
    terms = terms.reshape(2 * columns, share, hidden)
    terms = lax.all_to_all(
        terms, axes, split_axis=0, concat_axis=0, tiled=True, axis_index_groups=groups(second)
    )
    weight_grad, act = finish(terms, act)
    return (act, weight_grad)


def solution(mesh):
    n_feat, n_node = mesh.shape["feat"], mesh.shape["node"]
    fine = Mesh(
        mesh.devices.reshape(n_feat // 2, 2, n_node // 2, 2), ("col", "core", "hi", "lo")
    )
    feat, node = ("col", "core"), ("hi", "lo")
    return jax.shard_map(
        per_device,
        mesh=fine,
        in_specs=(
            P(feat, node),
            P(),
            P(feat, node, None),
            P(feat, node, None),
            P(feat, node, None),
            P(feat, node),
            P(feat, node, None, None, None),
            P(None, node + feat),
        ),
        out_specs=(P(None, node + feat), P(feat + node, None)),
        check_vma=False,
    )
```

```python
import functools

import jax
import jax.numpy as jnp
from jax import lax
from jax.experimental import pallas as pl
from jax.experimental.pallas import tpu as pltpu
from jax.sharding import Mesh, PartitionSpec as P

root_half = 0.7071067811865476
inv_root_two_pi = 0.3989422804014327

SWAP = ((0, 1), (1, 0))
TRANSPOSE = ((0, 0), (1, 2), (2, 1), (3, 3))
VMEM = pl.BlockSpec(memory_space=pltpu.VMEM)
SMEM = pl.BlockSpec(memory_space=pltpu.SMEM)
ANY = pl.BlockSpec(memory_space=pl.ANY)
PARAMS = pltpu.CompilerParams(vmem_limit_bytes=24 * 1024 * 1024)


def middle_first(columns, quarters=(2, 1, 0, 3)):
    quarter = max(columns // 4, 1)
    rest = sorted(range(columns), key=lambda column: -column)
    order = [column for at in quarters for column in rest if min(column // quarter, 3) == at]
    order.remove(columns // 2)
    return [columns // 2] + order


SECOND = (2, 1, 3, 0)


def dot(left, right, left_dim, right_dim):
    return lax.dot_general(
        left, right, (((left_dim,), (right_dim,)), ((), ())), preferred_element_type=jnp.float32
    )


def chunk_kernel(feats, chunks, held, in_sems, out_sems):
    places, columns, _, rows = chunks.shape
    for place in range(places):
        for at, column in enumerate(middle_first(columns)):
            source = (column * places + places - 1 - place) * rows
            pltpu.make_async_copy(
                feats.at[:, pl.ds(source, rows)], held.at[place, at], in_sems.at[place]
            ).start()
    stores = []
    for place in range(places):
        pltpu.make_async_copy(held.at[place], held.at[place], in_sems.at[place]).wait()
        stores.append(
            pltpu.make_async_copy(held.at[place], chunks.at[place], out_sems.at[place])
        )
        stores[-1].start()
    for store in stores:
        store.wait()


def by_destination(feats, places, columns):
    width, nodes = feats.shape
    shape = (places, columns, width, nodes // (places * columns))
    return pl.pallas_call(
        chunk_kernel,
        out_shape=jax.ShapeDtypeStruct(shape, feats.dtype),
        in_specs=[pl.BlockSpec(memory_space=pltpu.HBM)],
        out_specs=pl.BlockSpec(memory_space=pltpu.HBM),
        scratch_shapes=[
            pltpu.VMEM(shape, feats.dtype),
            pltpu.SemaphoreType.DMA((places,)),
            pltpu.SemaphoreType.DMA((places,)),
        ],
        compiler_params=pltpu.CompilerParams(vmem_limit_bytes=60 * 1024 * 1024),
        name="by_destination",
    )(feats)


def side_kernel(row_tile, col_tile, block_index, live, blocks, cotangent, out):
    slots, tile, _ = blocks.shape
    hidden, rows = cotangent.shape
    groups = out.shape[1] // rows
    part = hidden // groups
    for slot in range(slots):
        row = pl.multiple_of(row_tile[slot] * tile, tile)
        col = pl.multiple_of(col_tile[slot] * tile, tile)
        block = blocks[block_index[slot]]
        out[pl.ds(row, tile), pl.ds(col, tile)] = jnp.where(
            slot < live[...], block, jnp.zeros_like(block)
        )
    for group in range(groups):
        out[rows : rows + part, group * rows : (group + 1) * rows] = cotangent[
            group * part : (group + 1) * part, :
        ]


def side_inputs(row_tile, col_tile, block_index, live, blocks, cotangent):
    slots, tile, _ = blocks.shape
    hidden, rows = cotangent.shape
    cluster = slots * tile * tile // rows
    return pl.pallas_call(
        side_kernel,
        out_shape=jax.ShapeDtypeStruct((rows + hidden * rows // cluster, cluster), blocks.dtype),
        in_specs=[SMEM] * 3 + [VMEM] * 3,
        out_specs=VMEM,
        compiler_params=PARAMS,
        name="side_inputs",
    )(row_tile, col_tile, block_index, live, blocks, cotangent)


def project_kernel(weight, arrived, part, part_out):
    places, columns, width, rows = arrived.shape
    for place in range(places):
        nodes = arrived[places - 1 - place].reshape(columns * width, rows)
        value = dot(weight[...], nodes, 1, 0)
        part[:, place * rows : (place + 1) * rows] = value
        part_out[:, place * rows : (place + 1) * rows] = value.astype(part_out.dtype)


def project(weight, arrived):
    hidden = weight.shape[0]
    places, columns, width, rows = arrived.shape
    shape = (hidden, places * rows)
    return pl.pallas_call(
        project_kernel,
        out_shape=(
            jax.ShapeDtypeStruct(shape, jnp.float32),
            jax.ShapeDtypeStruct(shape, jnp.bfloat16),
        ),
        in_specs=[VMEM, VMEM],
        out_specs=(VMEM, VMEM),
        compiler_params=PARAMS,
        name="project",
    )(weight, arrived)


def parts(side, rows, hidden):
    groups = side.shape[1] // rows
    part = hidden // groups
    cotangent = jnp.concatenate(
        [side[rows : rows + part, group * rows : (group + 1) * rows] for group in range(groups)], 0
    )
    return side[:rows, :], cotangent


def block_grads(nodes, side, rows, act=None):
    adjacency, cotangent = parts(side, rows, nodes.shape[0])
    preact = dot(nodes, adjacency, 1, 1)
    normal_cdf = 0.5 * (1.0 + lax.erf(preact * root_half))
    normal_pdf = jnp.exp(-0.5 * preact * preact) * inv_root_two_pi
    if act is not None:
        act[...] = (preact * normal_cdf).astype(act.dtype)
    derivative = normal_cdf + preact * normal_pdf
    return (cotangent.astype(jnp.float32) * derivative).astype(jnp.bfloat16)


def block_terms(nodes, side, rows, act=None):
    return dot(block_grads(nodes, side, rows, act), side[:rows, :], 1, 0)


def spread_kernel(arrived, *refs):
    *sides, out = refs
    places, columns, width, rows = arrived.shape
    for at, side in enumerate(sides):
        total = None
        for place in range(places):
            nodes = arrived[places - 1 - place].reshape(columns * width, rows)
            value = dot(nodes, side[:rows, place * rows : (place + 1) * rows], 1, 1)
            total = value if total is None else total + value
        out[:, at * rows : (at + 1) * rows] = total.astype(out.dtype)


def spread(arrived, sides):
    _, columns, width, rows = arrived.shape
    shape = (columns * width, len(sides) * rows)
    return pl.pallas_call(
        spread_kernel,
        out_shape=jax.ShapeDtypeStruct(shape, arrived.dtype),
        in_specs=[VMEM] * (1 + len(sides)),
        out_specs=VMEM,
        compiler_params=PARAMS,
        cost_estimate=pl.CostEstimate(
            flops=4 * shape[0] * shape[1] * rows, bytes_accessed=4 * shape[0] * shape[1], transcendentals=0
        ),
        name="spread",
    )(arrived, *sides)


def gradient_terms(arrived, node_grad, terms, held, sems):
    places, columns, width, rows = arrived.shape
    count = held.shape[0]
    size = columns // count
    copies = []
    for group in range(count):
        total = None
        for place in range(places):
            source = places - 1 - place
            nodes = arrived[source, group * size : (group + 1) * size].reshape(size * width, rows)
            value = dot(nodes, node_grad[:, place * rows : (place + 1) * rows], 1, 1)
            total = value if total is None else total + value
        if len(terms.shape) == 2:
            held[group] = total
            target = terms.at[pl.ds(group * size * width, size * width)]
        else:
            share = terms.shape[2]
            total = total.astype(terms.dtype).reshape(size, places, share, total.shape[1])
            for place in range(places):
                held[group, places - 1 - place] = total[:, place]
            target = terms.at[:, pl.ds(group * size, size)]
        copies.append(pltpu.make_async_copy(held.at[group], target, sems.at[group]))
        copies[-1].start()
    for copy in copies:
        copy.wait()


def whole_kernel(part, other, own, pair, hidden, act, terms, held, sem):
    rows = act.shape[1]
    nodes = (part[...] + other[...].astype(jnp.float32)).astype(jnp.bfloat16)
    grads = [block_grads(nodes, own, rows, act), block_grads(nodes, pair, rows)]
    places, columns, share, units = held.shape
    count = 2
    size = columns // count
    order = middle_first(columns)
    rank = {column: at for at, column in enumerate(middle_first(columns, SECOND))}
    height = hidden.shape[0] // count
    for group in range(count):
        taken = hidden[group * height : (group + 1) * height, :]
        total = dot(taken[:, :rows], grads[0], 1, 1) + dot(taken[:, rows:], grads[1], 1, 1)
        total = total.astype(terms.dtype).reshape(size, places, share, units)
        for at in range(size):
            for place in range(places):
                held[places - 1 - place, rank[order[group * size + at]]] = total[at, place]
    copy = pltpu.make_async_copy(held, terms, sem)
    copy.start()
    copy.wait()


def node_kernel(nodes, own, pair, act, total):
    rows = act.shape[1]
    total[...] = block_terms(nodes[...], own, rows, act) + block_terms(nodes[...], pair, rows)


def gradient_kernel(arrived, node_grad, terms, held, sems):
    gradient_terms(arrived, node_grad[...], terms, held, sems)


def gradient_scratch(shape, dtype):
    count = 2
    if len(shape) == 2:
        held = (count, shape[0] // count, shape[1])
    else:
        held = (count, shape[0], shape[1] // count) + shape[2:]
    return [pltpu.VMEM(held, dtype), pltpu.SemaphoreType.DMA((count,))]


def whole(part, other, own, pair, hidden, rows, shape):
    act = jax.ShapeDtypeStruct((part.shape[0], rows), jnp.bfloat16)
    return pl.pallas_call(
        whole_kernel,
        out_shape=(act, jax.ShapeDtypeStruct(shape, jnp.bfloat16)),
        in_specs=[VMEM] * 5,
        out_specs=(VMEM, ANY),
        scratch_shapes=[pltpu.VMEM(shape, jnp.bfloat16), pltpu.SemaphoreType.DMA],
        compiler_params=PARAMS,
        name="blocks_and_gradient",
    )(part, other, own, pair, hidden)


def node_sums(nodes, own, pair, rows):
    act = jax.ShapeDtypeStruct((nodes.shape[0], rows), jnp.bfloat16)
    return pl.pallas_call(
        node_kernel,
        out_shape=(act, jax.ShapeDtypeStruct(nodes.shape, jnp.float32)),
        in_specs=[VMEM] * 3,
        out_specs=(VMEM, VMEM),
        compiler_params=PARAMS,
        name="block",
    )(nodes, own, pair)


def gradient(arrived, node_grad, shape):
    return pl.pallas_call(
        gradient_kernel,
        out_shape=jax.ShapeDtypeStruct(shape, jnp.float32),
        in_specs=[VMEM] * 2,
        out_specs=ANY,
        scratch_shapes=gradient_scratch(shape, jnp.float32),
        compiler_params=PARAMS,
        name="gradient",
    )(arrived, node_grad)


def finish_kernel(terms, act, total_out, act_out, total, sems):
    act_copy = pltpu.make_async_copy(act, act_out, sems.at[0])
    act_copy.start()
    total[...] = jnp.sum(terms[...].astype(jnp.float32), axis=0)
    total_copy = pltpu.make_async_copy(total, total_out, sems.at[1])
    total_copy.start()
    act_copy.wait()
    total_copy.wait()


def finish(terms, act):
    return pl.pallas_call(
        finish_kernel,
        out_shape=(
            jax.ShapeDtypeStruct(terms.shape[1:], jnp.float32),
            jax.ShapeDtypeStruct(act.shape, act.dtype),
        ),
        in_specs=[VMEM, ANY],
        out_specs=(ANY, ANY),
        scratch_shapes=[
            pltpu.VMEM(terms.shape[1:], jnp.float32),
            pltpu.SemaphoreType.DMA((2,)),
        ],
        compiler_params=PARAMS,
        name="finish",
    )(terms, act)


def per_device(feats, weight, tile_row, tile_col, tile_block, tile_count, edge_blocks, cotangent):
    columns = lax.axis_size("col")
    pairs = lax.axis_size("hi")
    core = lax.axis_index("core")
    width, shard_nodes = feats.shape
    rows = shard_nodes // (2 * columns)
    hidden = weight.shape[1]
    bf16 = jnp.bfloat16
    order = middle_first(columns)
    axes = ("col", "core", "hi", "lo")

    def groups(listed):
        return [
            [((column * 2 + c) * pairs + hi) * 2 + place for place in (1, 0) for column in listed]
            for c in range(2)
            for hi in range(pairs)
        ]

    second = middle_first(columns, SECOND)

    chunks = by_destination(feats, 2, columns).reshape(2 * columns, width, rows)
    arrived = lax.all_to_all(
        chunks, axes, split_axis=0, concat_axis=0, tiled=True, axis_index_groups=groups(order)
    )
    arrived = arrived.reshape(2, columns, width, rows)

    side = side_inputs(
        tile_row[0, 0], tile_col[0, 0], tile_block[0, 0], tile_count, edge_blocks[0, 0], cotangent
    )
    side = lax.ppermute(side, ("core", "lo"), TRANSPOSE)
    own_weight = lax.dynamic_index_in_dim(
        weight.reshape(columns, 2, width, hidden), core, 1, keepdims=False
    )
    own_weight = jnp.stack([own_weight[column] for column in order])
    own_weight = own_weight.reshape(columns * width, hidden).T
    arrived, side, own_weight = lax.optimization_barrier((arrived, side, own_weight))
    side_pair = lax.ppermute(side, "core", SWAP)

    part, sent = project(own_weight, arrived)
    sent, arrived = lax.optimization_barrier((sent, arrived))
    other = lax.ppermute(sent, "core", SWAP)
    share = width // (2 * pairs)
    if pairs > 1:
        nodes = (part + other.astype(jnp.float32)).astype(bf16)
        nodes = lax.all_gather(nodes, "hi", axis=1, tiled=True)
        output, node_grad = node_sums(nodes, side, side_pair, rows)
        node_grad = lax.psum_scatter(node_grad, "hi", scatter_dimension=1, tiled=True)
        terms = gradient(arrived, node_grad.astype(bf16), (columns * width, hidden))
        terms = terms.reshape(columns, pairs, 2, share, hidden)
        terms = lax.psum_scatter(terms, "hi", scatter_dimension=1, tiled=True).astype(bf16)
        terms = jnp.stack([terms[order.index(column), 0, ::-1] for column in second], 1)
    else:
        summed = spread(arrived, (side, side_pair))
        output, terms = whole(
            part, other, side, side_pair, summed, rows, (2, columns, share, hidden)
        )
    act = lax.ppermute(output, ("core", "lo"), TRANSPOSE)
    terms = terms.reshape(2 * columns, share, hidden)
    terms = lax.all_to_all(
        terms, axes, split_axis=0, concat_axis=0, tiled=True, axis_index_groups=groups(second)
    )
    weight_grad, act = finish(terms, act)
    return (act, weight_grad)


def solution(mesh):
    n_feat, n_node = mesh.shape["feat"], mesh.shape["node"]
    fine = Mesh(
        mesh.devices.reshape(n_feat // 2, 2, n_node // 2, 2), ("col", "core", "hi", "lo")
    )
    feat, node = ("col", "core"), ("hi", "lo")
    return jax.shard_map(
        per_device,
        mesh=fine,
        in_specs=(
            P(feat, node),
            P(),
            P(feat, node, None),
            P(feat, node, None),
            P(feat, node, None),
            P(feat, node),
            P(feat, node, None, None, None),
            P(None, node + feat),
        ),
        out_specs=(P(None, node + feat), P(feat + node, None)),
        check_vma=False,
    )
```

```python
import functools

import jax
import jax.numpy as jnp
from jax import lax
from jax.experimental import pallas as pl
from jax.experimental.pallas import tpu as pltpu
from jax.sharding import Mesh, PartitionSpec as P

root_half = 0.7071067811865476
inv_root_two_pi = 0.3989422804014327

SWAP = ((0, 1), (1, 0))
TRANSPOSE = ((0, 0), (1, 2), (2, 1), (3, 3))
VMEM = pl.BlockSpec(memory_space=pltpu.VMEM)
SMEM = pl.BlockSpec(memory_space=pltpu.SMEM)
ANY = pl.BlockSpec(memory_space=pl.ANY)
PARAMS = pltpu.CompilerParams(vmem_limit_bytes=24 * 1024 * 1024)


def middle_first(columns, quarters=(2, 1, 0, 3)):
    quarter = max(columns // 4, 1)
    rest = sorted(range(columns), key=lambda column: -column)
    order = [column for at in quarters for column in rest if min(column // quarter, 3) == at]
    order.remove(columns // 2)
    return [columns // 2] + order


SECOND = (2, 1, 3, 0)


def dot(left, right, left_dim, right_dim):
    return lax.dot_general(
        left, right, (((left_dim,), (right_dim,)), ((), ())), preferred_element_type=jnp.float32
    )


def chunk_kernel(feats, chunks, held, in_sems, out_sems):
    places, columns, _, rows = chunks.shape
    for place in range(places):
        for at, column in enumerate(middle_first(columns)):
            source = (column * places + places - 1 - place) * rows
            pltpu.make_async_copy(
                feats.at[:, pl.ds(source, rows)], held.at[place, at], in_sems.at[place]
            ).start()
    stores = []
    for place in range(places):
        pltpu.make_async_copy(held.at[place], held.at[place], in_sems.at[place]).wait()
        stores.append(
            pltpu.make_async_copy(held.at[place], chunks.at[place], out_sems.at[place])
        )
        stores[-1].start()
    for store in stores:
        store.wait()


def by_destination(feats, places, columns):
    width, nodes = feats.shape
    shape = (places, columns, width, nodes // (places * columns))
    return pl.pallas_call(
        chunk_kernel,
        out_shape=jax.ShapeDtypeStruct(shape, feats.dtype),
        in_specs=[pl.BlockSpec(memory_space=pltpu.HBM)],
        out_specs=pl.BlockSpec(memory_space=pltpu.HBM),
        scratch_shapes=[
            pltpu.VMEM(shape, feats.dtype),
            pltpu.SemaphoreType.DMA((places,)),
            pltpu.SemaphoreType.DMA((places,)),
        ],
        compiler_params=pltpu.CompilerParams(vmem_limit_bytes=60 * 1024 * 1024),
        name="by_destination",
    )(feats)


def side_kernel(row_tile, col_tile, block_index, live, blocks, cotangent, out):
    slots, tile, _ = blocks.shape
    hidden, rows = cotangent.shape
    groups = out.shape[1] // rows
    part = hidden // groups
    for slot in range(slots):
        row = pl.multiple_of(row_tile[slot] * tile, tile)
        col = pl.multiple_of(col_tile[slot] * tile, tile)
        block = blocks[block_index[slot]]
        out[pl.ds(row, tile), pl.ds(col, tile)] = jnp.where(
            slot < live[0], block, jnp.zeros_like(block)
        )
    for group in range(groups):
        out[rows : rows + part, group * rows : (group + 1) * rows] = cotangent[
            group * part : (group + 1) * part, :
        ]


def side_inputs(row_tile, col_tile, block_index, live, blocks, cotangent):
    slots, tile, _ = blocks.shape
    hidden, rows = cotangent.shape
    cluster = slots * tile * tile // rows
    return pl.pallas_call(
        side_kernel,
        out_shape=jax.ShapeDtypeStruct((rows + hidden * rows // cluster, cluster), blocks.dtype),
        in_specs=[SMEM] * 4 + [VMEM] * 2,
        out_specs=VMEM,
        compiler_params=PARAMS,
        name="side_inputs",
    )(row_tile, col_tile, block_index, live, blocks, cotangent)


def project_kernel(weight, arrived, part, part_out):
    places, columns, width, rows = arrived.shape
    for place in range(places):
        nodes = arrived[places - 1 - place].reshape(columns * width, rows)
        value = dot(weight[...], nodes, 1, 0)
        part[:, place * rows : (place + 1) * rows] = value
        part_out[:, place * rows : (place + 1) * rows] = value.astype(part_out.dtype)


def project(weight, arrived):
    hidden = weight.shape[0]
    places, columns, width, rows = arrived.shape
    shape = (hidden, places * rows)
    return pl.pallas_call(
        project_kernel,
        out_shape=(
            jax.ShapeDtypeStruct(shape, jnp.float32),
            jax.ShapeDtypeStruct(shape, jnp.bfloat16),
        ),
        in_specs=[VMEM, VMEM],
        out_specs=(VMEM, VMEM),
        compiler_params=PARAMS,
        name="project",
    )(weight, arrived)


def parts(side, rows, hidden):
    groups = side.shape[1] // rows
    part = hidden // groups
    cotangent = jnp.concatenate(
        [side[rows : rows + part, group * rows : (group + 1) * rows] for group in range(groups)], 0
    )
    return side[:rows, :], cotangent


def block_grads(nodes, side, rows, act=None):
    adjacency, cotangent = parts(side, rows, nodes.shape[0])
    preact = dot(nodes, adjacency, 1, 1)
    normal_cdf = 0.5 * (1.0 + lax.erf(preact * root_half))
    normal_pdf = jnp.exp(-0.5 * preact * preact) * inv_root_two_pi
    if act is not None:
        act[...] = (preact * normal_cdf).astype(act.dtype)
    derivative = normal_cdf + preact * normal_pdf
    return (cotangent.astype(jnp.float32) * derivative).astype(jnp.bfloat16)


def block_terms(nodes, side, rows, act=None):
    return dot(block_grads(nodes, side, rows, act), side[:rows, :], 1, 0)


def spread_kernel(arrived, *refs):
    *sides, out = refs
    places, columns, width, rows = arrived.shape
    for at, side in enumerate(sides):
        total = None
        for place in range(places):
            nodes = arrived[places - 1 - place].reshape(columns * width, rows)
            value = dot(nodes, side[:rows, place * rows : (place + 1) * rows], 1, 1)
            total = value if total is None else total + value
        out[:, at * rows : (at + 1) * rows] = total.astype(out.dtype)


def spread(arrived, sides):
    _, columns, width, rows = arrived.shape
    shape = (columns * width, len(sides) * rows)
    return pl.pallas_call(
        spread_kernel,
        out_shape=jax.ShapeDtypeStruct(shape, arrived.dtype),
        in_specs=[VMEM] * (1 + len(sides)),
        out_specs=VMEM,
        compiler_params=PARAMS,
        cost_estimate=pl.CostEstimate(
            flops=4 * shape[0] * shape[1] * rows, bytes_accessed=4 * shape[0] * shape[1], transcendentals=0
        ),
        name="spread",
    )(arrived, *sides)


def gradient_terms(arrived, node_grad, terms, held, sems):
    places, columns, width, rows = arrived.shape
    count = held.shape[0]
    size = columns // count
    copies = []
    for group in range(count):
        total = None
        for place in range(places):
            source = places - 1 - place
            nodes = arrived[source, group * size : (group + 1) * size].reshape(size * width, rows)
            value = dot(nodes, node_grad[:, place * rows : (place + 1) * rows], 1, 1)
            total = value if total is None else total + value
        if len(terms.shape) == 2:
            held[group] = total
            target = terms.at[pl.ds(group * size * width, size * width)]
        else:
            share = terms.shape[2]
            total = total.astype(terms.dtype).reshape(size, places, share, total.shape[1])
            for place in range(places):
                held[group, places - 1 - place] = total[:, place]
            target = terms.at[:, pl.ds(group * size, size)]
        copies.append(pltpu.make_async_copy(held.at[group], target, sems.at[group]))
        copies[-1].start()
    for copy in copies:
        copy.wait()


def whole_kernel(part, other, own, pair, hidden, act, terms, held, sem):
    rows = act.shape[1]
    nodes = (part[...] + other[...].astype(jnp.float32)).astype(jnp.bfloat16)
    grads = jnp.concatenate(
        [block_grads(nodes, own, rows, act), block_grads(nodes, pair, rows)], 1
    )
    places, columns, share, units = held.shape
    count = 2
    size = columns // count
    order = middle_first(columns)
    rank = {column: at for at, column in enumerate(middle_first(columns, SECOND))}
    height = hidden.shape[0] // count
    for group in range(count):
        taken = hidden[group * height : (group + 1) * height, :]
        total = dot(taken, grads, 1, 1)
        total = total.astype(terms.dtype).reshape(size, places, share, units)
        for at in range(size):
            for place in range(places):
                held[places - 1 - place, rank[order[group * size + at]]] = total[at, place]
    copy = pltpu.make_async_copy(held, terms, sem)
    copy.start()
    copy.wait()


def node_kernel(nodes, own, pair, act, total):
    rows = act.shape[1]
    total[...] = block_terms(nodes[...], own, rows, act) + block_terms(nodes[...], pair, rows)


def gradient_kernel(arrived, node_grad, terms, held, sems):
    gradient_terms(arrived, node_grad[...], terms, held, sems)


def gradient_scratch(shape, dtype):
    count = 2
    if len(shape) == 2:
        held = (count, shape[0] // count, shape[1])
    else:
        held = (count, shape[0], shape[1] // count) + shape[2:]
    return [pltpu.VMEM(held, dtype), pltpu.SemaphoreType.DMA((count,))]


def whole(part, other, own, pair, hidden, rows, shape):
    act = jax.ShapeDtypeStruct((part.shape[0], rows), jnp.bfloat16)
    return pl.pallas_call(
        whole_kernel,
        out_shape=(act, jax.ShapeDtypeStruct(shape, jnp.bfloat16)),
        in_specs=[VMEM] * 5,
        out_specs=(VMEM, ANY),
        scratch_shapes=[pltpu.VMEM(shape, jnp.bfloat16), pltpu.SemaphoreType.DMA],
        compiler_params=PARAMS,
        name="blocks_and_gradient",
    )(part, other, own, pair, hidden)


def node_sums(nodes, own, pair, rows):
    act = jax.ShapeDtypeStruct((nodes.shape[0], rows), jnp.bfloat16)
    return pl.pallas_call(
        node_kernel,
        out_shape=(act, jax.ShapeDtypeStruct(nodes.shape, jnp.float32)),
        in_specs=[VMEM] * 3,
        out_specs=(VMEM, VMEM),
        compiler_params=PARAMS,
        name="block",
    )(nodes, own, pair)


def gradient(arrived, node_grad, shape):
    return pl.pallas_call(
        gradient_kernel,
        out_shape=jax.ShapeDtypeStruct(shape, jnp.float32),
        in_specs=[VMEM] * 2,
        out_specs=ANY,
        scratch_shapes=gradient_scratch(shape, jnp.float32),
        compiler_params=PARAMS,
        name="gradient",
    )(arrived, node_grad)


def finish_kernel(terms, act, total_out, act_out, total, sems):
    act_copy = pltpu.make_async_copy(act, act_out, sems.at[0])
    act_copy.start()
    total[...] = jnp.sum(terms[...].astype(jnp.float32), axis=0)
    total_copy = pltpu.make_async_copy(total, total_out, sems.at[1])
    total_copy.start()
    act_copy.wait()
    total_copy.wait()


def finish(terms, act):
    return pl.pallas_call(
        finish_kernel,
        out_shape=(
            jax.ShapeDtypeStruct(terms.shape[1:], jnp.float32),
            jax.ShapeDtypeStruct(act.shape, act.dtype),
        ),
        in_specs=[VMEM, ANY],
        out_specs=(ANY, ANY),
        scratch_shapes=[
            pltpu.VMEM(terms.shape[1:], jnp.float32),
            pltpu.SemaphoreType.DMA((2,)),
        ],
        compiler_params=PARAMS,
        name="finish",
    )(terms, act)


def per_device(feats, weight, tile_row, tile_col, tile_block, tile_count, edge_blocks, cotangent):
    columns = lax.axis_size("col")
    pairs = lax.axis_size("hi")
    core = lax.axis_index("core")
    width, shard_nodes = feats.shape
    rows = shard_nodes // (2 * columns)
    hidden = weight.shape[1]
    bf16 = jnp.bfloat16
    order = middle_first(columns)
    axes = ("col", "core", "hi", "lo")

    def groups(listed):
        return [
            [((column * 2 + c) * pairs + hi) * 2 + place for place in (1, 0) for column in listed]
            for c in range(2)
            for hi in range(pairs)
        ]

    second = middle_first(columns, SECOND)

    chunks = by_destination(feats, 2, columns).reshape(2 * columns, width, rows)
    arrived = lax.all_to_all(
        chunks, axes, split_axis=0, concat_axis=0, tiled=True, axis_index_groups=groups(order)
    )
    arrived = arrived.reshape(2, columns, width, rows)

    side = side_inputs(
        tile_row[0, 0], tile_col[0, 0], tile_block[0, 0], tile_count[0], edge_blocks[0, 0], cotangent
    )
    side = lax.ppermute(side, ("core", "lo"), TRANSPOSE)
    own_weight = lax.dynamic_index_in_dim(
        weight.reshape(columns, 2, width, hidden), core, 1, keepdims=False
    )
    own_weight = jnp.stack([own_weight[column] for column in order])
    own_weight = own_weight.reshape(columns * width, hidden).T
    arrived, side, own_weight = lax.optimization_barrier((arrived, side, own_weight))
    side_pair = lax.ppermute(side, "core", SWAP)

    part, sent = project(own_weight, arrived)
    sent, arrived = lax.optimization_barrier((sent, arrived))
    other = lax.ppermute(sent, "core", SWAP)
    share = width // (2 * pairs)
    if pairs > 1:
        nodes = (part + other.astype(jnp.float32)).astype(bf16)
        nodes = lax.all_gather(nodes, "hi", axis=1, tiled=True)
        output, node_grad = node_sums(nodes, side, side_pair, rows)
        node_grad = lax.psum_scatter(node_grad, "hi", scatter_dimension=1, tiled=True)
        terms = gradient(arrived, node_grad.astype(bf16), (columns * width, hidden))
        terms = terms.reshape(columns, pairs, 2, share, hidden)
        terms = lax.psum_scatter(terms, "hi", scatter_dimension=1, tiled=True).astype(bf16)
        terms = jnp.stack([terms[order.index(column), 0, ::-1] for column in second], 1)
    else:
        summed = spread(arrived, (side, side_pair))
        output, terms = whole(
            part, other, side, side_pair, summed, rows, (2, columns, share, hidden)
        )
    act = lax.ppermute(output, ("core", "lo"), TRANSPOSE)
    terms = terms.reshape(2 * columns, share, hidden)
    terms = lax.all_to_all(
        terms, axes, split_axis=0, concat_axis=0, tiled=True, axis_index_groups=groups(second)
    )
    weight_grad, act = finish(terms, act)
    return (act, weight_grad)


def solution(mesh):
    n_feat, n_node = mesh.shape["feat"], mesh.shape["node"]
    fine = Mesh(
        mesh.devices.reshape(n_feat // 2, 2, n_node // 2, 2), ("col", "core", "hi", "lo")
    )
    feat, node = ("col", "core"), ("hi", "lo")
    return jax.shard_map(
        per_device,
        mesh=fine,
        in_specs=(
            P(feat, node),
            P(),
            P(feat, node, None),
            P(feat, node, None),
            P(feat, node, None),
            P(feat, node),
            P(feat, node, None, None, None),
            P(None, node + feat),
        ),
        out_specs=(P(None, node + feat), P(feat + node, None)),
        check_vma=False,
    )
```
